512 devices in a mesh: wide: 64 (over z_lo, y, core), narrow: 8 (over z_hi, x).
Axes of the slice: x: 4, y: 8, z: 8 (z_hi: 2, z_lo: 4; z = z_hi * 4 + z_lo), core: 2. Of those that a mesh axis runs over, the one named last changes fastest.
Arguments:
- density: bfloat16 [128, 64, 32, 192], P('wide', 'narrow'), may hold values from -6 to 6
- analysis_weight: bfloat16 [5, 5, 5, 192, 192], P(None, None, None, 'narrow'), may hold values from -0.0390625 to 0.0390625
- analysis_bias: float32 [192], replicated, may hold values from -3 to 3
- norm_beta: float32 [192], replicated, may hold values from 0.5 to 2
- norm_gamma: float32 [192, 192], replicated, may hold values from 0.0001 to 0.1
- hyper_weight: bfloat16 [3, 3, 3, 192, 192], P(None, None, None, 'narrow'), may hold values from -0.078125 to 0.078125
- hyper_bias: float32 [192], replicated, may hold values from -3 to 3
- synthesis_weight: bfloat16 [3, 3, 3, 192, 192], P(None, None, None, 'narrow'), may hold values from -0.078125 to 0.078125
- synthesis_bias: float32 [192], replicated, may hold values from -4 to 4
Outputs:
- latent: bfloat16 [64, 32, 16, 192], P('wide', 'narrow')
- scales: float32 [64, 32, 16, 192], P('wide', 'narrow')
The draws below stay inside these ranges and needn't reach their ends.
All inputs are finite; a program needn't handle non-finite values.
Results may differ from the reference program's by a relative error of at most 0.0034.
Values may be sent and summed in bfloat16 or wider, within the bound.
A program may use at most 64 MiB of HBM per device.

```python
import math
import jax
import jax.numpy as jnp
from jax import lax

C = 192
PLANES = 128
ROWS = 64
COLS = 32


def shard_levels(key, extent, split, low, top_value):
    factor_of, own = 1.0, jax.random.fold_in(key, 6)
    for axis_at, parts in split:
        draws = jnp.exp(jax.random.uniform(jax.random.fold_in(own, axis_at), (parts,), jnp.float32, low / len(split), top_value / len(split)))
        factor_of = factor_of * jnp.repeat(draws, extent[axis_at] // parts).reshape([-1 if axis == axis_at else 1 for axis in range(len(extent))])
    return factor_of


def noise(key, shape, spread, most, cuts=(), kind=jnp.bfloat16):
    gain = shard_levels(key, shape, cuts, -0.22, 0.18) if cuts else 1.0
    array = jax.random.normal(key, shape, jnp.float32) * spread * gain
    return jnp.minimum(jnp.maximum(array, -most), most).astype(kind)


def setup_inputs(seed: int = 0) -> dict:
    key_of = jax.random.split(jax.random.key(seed), 10)
    density = noise(key_of[0], (PLANES, ROWS, COLS, C), 1.0, 6.0, ((0, 64), (1, 8)))
    analysis_weight = noise(key_of[1], (5, 5, 5, C, C), (125 * C) ** -0.5, 0.0390625, ((3, 8),))
    analysis_bias = noise(key_of[2], (C,), 0.5, 3.0, (), jnp.float32)
    norm_beta = jnp.clip(jnp.exp(jax.random.uniform(key_of[3], (C,), jnp.float32, math.log(0.5), math.log(2.0))), 0.5, 2.0)
    norm_gamma = jnp.clip(jnp.exp(jax.random.uniform(key_of[4], (C, C), jnp.float32, math.log(0.0001), math.log(0.1))), 0.0001, 0.1)
    hyper_weight = noise(key_of[5], (3, 3, 3, C, C), (27 * C) ** -0.5, 0.078125, ((3, 8),))
    hyper_bias = noise(key_of[6], (C,), 0.5, 3.0, (), jnp.float32)
    synthesis_weight = noise(key_of[7], (3, 3, 3, C, C), (27 * C) ** -0.5, 0.078125, ((3, 8),))
    synthesis_bias = noise(key_of[8], (C,), 1.0, 4.0, (), jnp.float32)
    return {"density": density, "analysis_weight": analysis_weight, "analysis_bias": analysis_bias, "norm_beta": norm_beta, "norm_gamma": norm_gamma, "hyper_weight": hyper_weight, "hyper_bias": hyper_bias, "synthesis_weight": synthesis_weight, "synthesis_bias": synthesis_bias}


def normalize(conv_out, norm_beta, norm_gamma):
    denom = norm_beta + jnp.dot(conv_out * conv_out, norm_gamma, precision=lax.Precision.HIGHEST)
    return conv_out * lax.rsqrt(denom)

def analysis_conv(density, weight):
    padded = jnp.pad(density, ((2, 2), (2, 2), (2, 2), (0, 0)))
    weight_full = weight.astype(jnp.float32)
    count = density.shape[0] // 2

    def one_plane(index):
        block = lax.dynamic_slice_in_dim(padded, 2 * index, 5, 0).astype(jnp.float32)
        result = lax.conv_general_dilated(block[None], weight_full, (2, 2, 2), 'VALID', dimension_numbers=('NDHWC', 'DHWIO', 'NDHWC'), precision=lax.Precision.HIGHEST)
        return result[0, 0]
    return lax.map(one_plane, jnp.arange(count, dtype=jnp.int32))

def cube_conv(values, weight):
    result = lax.conv_general_dilated(values.astype(jnp.float32)[None], weight.astype(jnp.float32), (1, 1, 1), ((1, 1), (1, 1), (1, 1)), dimension_numbers=('NDHWC', 'DHWIO', 'NDHWC'), precision=lax.Precision.HIGHEST)
    return result[0]

def reference(density, analysis_weight, analysis_bias, norm_beta, norm_gamma, hyper_weight, hyper_bias, synthesis_weight, synthesis_bias):
    conv_out = analysis_conv(density, analysis_weight) + analysis_bias
    latent = normalize(conv_out, norm_beta, norm_gamma).astype(jnp.bfloat16)
    hidden = jax.nn.relu(cube_conv(jnp.abs(latent), hyper_weight) + hyper_bias).astype(jnp.bfloat16)
    scales = 0.11 + jax.nn.softplus(cube_conv(hidden, synthesis_weight) + synthesis_bias)
    return (latent, scales)
```

```python
import jax
import jax.numpy as jnp
from jax import lax
from jax.experimental import pallas as pl
from jax.experimental.pallas import tpu as pltpu
from jax.sharding import PartitionSpec as P

MESH = pl.DeviceIdType.MESH
F32 = jnp.float32
BF16 = jnp.bfloat16

FAR = ((1, 2), (1, 1), (1, 3), (1, 0))
NEAR = ((0, 2), (0, 1), (0, 3))
TAPS = tuple((a, b, c) for a in range(3) for b in range(3) for c in range(3))


def iota(shape, dim):
    return lax.broadcasted_iota(jnp.int32, shape, dim)


def rows_shifted(x, by):
    n = x.shape[0]
    col = iota(x.shape, 0) & 15
    if by == -1:
        return jnp.where(col == 0, 0.0, pltpu.roll(x, 1, 0))
    return jnp.where(col == 15, 0.0, pltpu.roll(x, n - 1, 0))


def kernel(
    x_ref, w1_ref, b1_ref, beta_ref, gamma_ref, w2_ref, b2_ref, w3_ref, b3_ref,
    lat_ref, sc_ref,
    send1, recv1, from_lo, from_hi, planes, w1k, acc, send2, recv2, wts,
    lat_p, lat_q, hid_p, hid_q,
    s1_send, s1_recv, f_send, f_recv, s2_send, s2_recv,
    g_send, g_recv, c_send, c_recv, l_send, l_recv, h_send, h_recv,
):
    w, n = lax.axis_index("wide"), lax.axis_index("narrow")
    wide = lax.axis_size("wide")
    zh, xx, core = n // 4, n % 4, w % 2
    has_lo, has_hi = w > 0, w < wide - 1
    lo, hi = jnp.maximum(w - 1, 0), jnp.minimum(w + 1, wide - 1)
    sibling = w + 1 - 2 * core

    def peer(e, d):
        return ((zh + e) % 2) * 4 + (xx + d) % 4

    sent = []

    def send(src, dst, ssem, rsem, device, when=None):
        copy = pltpu.make_async_remote_copy(
            src_ref=src, dst_ref=dst, send_sem=ssem, recv_sem=rsem,
            device_id=device, device_id_type=MESH,
        )
        if when is None:
            copy.start()
        else:
            pl.when(when)(copy.start)
        sent.append((copy, when))

    def arrived(dst, rsem, when=None):
        copy = pltpu.make_async_remote_copy(
            src_ref=dst, dst_ref=dst, send_sem=rsem, recv_sem=rsem,
            device_id=(sibling, n), device_id_type=MESH,
        )
        if when is None:
            copy.wait_recv()
        else:
            pl.when(when)(copy.wait_recv)

    barrier = pltpu.get_barrier_semaphore()
    for e, d in FAR + NEAR:
        pl.semaphore_signal(barrier, inc=1, device_id=(w, peer(e, d)), device_id_type=MESH)

    @pl.when(has_lo)
    def _():
        pl.semaphore_signal(barrier, inc=1, device_id=(lo, n), device_id_type=MESH)

    @pl.when(has_hi)
    def _():
        pl.semaphore_signal(barrier, inc=1, device_id=(hi, n), device_id_type=MESH)

    i, j = iota((256, 256), 0), iota((256, 256), 1)
    source = ((i >> 4) & 3) * 64 + (i >> 7) * 32 + (i & 15) * 2 + ((i >> 6) & 1)
    perm = jnp.where(j == source, 1.0, 0.0).astype(BF16)
    cut = [
        jnp.dot(perm, x_ref[256 * z : 256 * z + 256, :], preferred_element_type=F32).astype(BF16)
        for z in range(2)
    ]
    parts = [
        jnp.concatenate([cut[z][64 * t : 64 * t + 64] for z in range(2)], axis=0) for t in range(4)
    ]
    k, l = iota((192, 256), 0), iota((192, 256), 1)
    lane, which = l & 127, l >> 7
    for pair in range(4):
        total = jnp.zeros((128, 256), F32)
        for t in range(4):
            inside = (lane >= 24 * t) & (lane < 24 * t + 24)
            pick = inside & (k == 24 * (2 * pair + which) + lane - 24 * t)
            pick = jnp.where(pick, 1.0, 0.0).astype(BF16)
            total = total + jnp.dot(parts[t], pick, preferred_element_type=F32)
        total = total.astype(BF16)
        for side in range(2):
            for z in range(2):
                send1[2 * pair + side, z] = total[64 * z : 64 * z + 64, 128 * side : 128 * side + 128]

    own_rows = pl.ds(pl.multiple_of(32 * n, 32), 32)
    for layer, ref in ((0, w2_ref), (1, w3_ref)):

        @pl.loop(0, 7)
        def _(t, layer=layer, ref=ref):
            tap = 14 * core + 2 * t
            blank = jnp.zeros((8, 192), F32)
            even = ref[tap].astype(F32)
            odd = ref[jnp.minimum(tap + 1, 26)].astype(F32)
            odd = jnp.where(tap + 1 < 27, odd, 0.0)
            even = jnp.concatenate([even, blank], axis=0)
            odd = jnp.concatenate([odd, blank], axis=0)
            at = 21 * core + 3 * t
            wts[layer, at, own_rows, :] = even[:, :128].astype(BF16)
            wts[layer, at + 1, own_rows, :] = odd[:, :128].astype(BF16)
            both = jnp.concatenate([even[:, 128:], odd[:, 128:]], axis=1)
            wts[layer, at + 2, own_rows, :] = both.astype(BF16)

    pl.semaphore_wait(barrier, 7 + has_lo.astype(jnp.int32) + has_hi.astype(jnp.int32))

    for e, d in FAR + NEAR:
        m = peer(e, d)
        send(send1.at[m], recv1.at[n], s1_send.at[m], s1_recv.at[n], (w, m))
    recv1[n] = send1[n]

    half = pl.ds(21 * core, 21)

    def slice_of(layer, m):
        return wts.at[layer, half, pl.ds(pl.multiple_of(32 * m, 32), 32), :]

    mirror = peer(1, 0)
    for layer in range(2):
        for at, (e, d) in enumerate(((1, 0),) + NEAR):
            m = peer(e, d)
            part = slice_of(layer, n)
            send(part, part, g_send.at[layer, at], g_recv.at[layer, n], (w, m))

    w1k[...] = jnp.zeros_like(w1k)

    @pl.loop(0, 5)
    def _(a):
        for b in range(5):
            step, rp = b // 2, b % 2
            at = a * 3 + step
            v = w1_ref[a * 5 + b].astype(F32)
            last = jnp.concatenate([v[96:120], jnp.zeros((8, 192), F32)], axis=0)
            w1k[at, 48 * rp : 48 * rp + 48, 0:192] = v[0:48].astype(BF16)
            w1k[at, 128 + 48 * rp : 176 + 48 * rp, 0:192] = v[48:96].astype(BF16)
            w1k[at, 96 + 128 * rp : 128 + 128 * rp, 0:192] = last.astype(BF16)

    planes[:, 0:16, :] = jnp.zeros((5, 16, 256), BF16)
    planes[:, 528:544, :] = jnp.zeros((5, 16, 256), BF16)
    acc[0:32, :] = jnp.zeros((32, 256), F32)
    acc[544:576, :] = jnp.zeros((32, 256), F32)

    for turn in range(2):
        for e, d in NEAR if turn == 0 else FAR:
            m = peer(e, d)
            arrived(recv1.at[m], s1_recv.at[m])
        g = (zh + turn) % 2
        four = pl.ds(4 * g, 4)
        send(recv1.at[four], from_lo.at[four], f_send.at[0, turn], f_recv.at[0, g], (hi, n), has_hi)
        send(
            recv1.at[four, 0], from_hi.at[four], f_send.at[1, turn], f_recv.at[1, g], (lo, n), has_lo
        )

    def build(a, read):
        @pl.loop(0, 8)
        def _(blk):
            x = read(blk).astype(F32)
            ln = iota(x.shape, 1)
            after = rows_shifted(x, 1)
            before = jnp.where(ln < 96, rows_shifted(x, -1), pltpu.roll(after, 96, 1))
            same = jnp.where(ln < 96, x, pltpu.roll(after, 48, 1))
            at = pl.ds(pl.multiple_of(16 + 64 * blk, 16), 64)
            planes[a, at, 0:128] = before.astype(BF16)
            planes[a, at, 128:256] = same.astype(BF16)

    def product(a):
        rows = jnp.concatenate([planes[a, 16 * s : 16 * s + 512, :] for s in range(3)], axis=1)
        return jnp.dot(
            rows, w1k[3 * a : 3 * a + 3].reshape(768, 256), preferred_element_type=F32
        )

    build(2, lambda blk: recv1[blk, 0])
    build(3, lambda blk: recv1[blk, 1])
    acc[32:544, :] = product(2)
    acc[32:544, :] += product(3)

    def forward(layer):
        part = slice_of(layer, mirror)
        arrived(part, g_recv.at[layer, mirror])
        for at, (e, d) in enumerate(NEAR):
            send(part, part, g_send.at[layer, 4 + at], g_recv.at[layer, mirror], (w, peer(e, d)))

    def to_sibling(layer):
        for e, d in NEAR + FAR[:3]:
            m = peer(e, d)
            arrived(slice_of(layer, m), g_recv.at[layer, m])
        part = wts.at[layer, half]
        send(part, part, c_send.at[layer], c_recv.at[layer], (sibling, n))

    forward(0)

    @pl.when(jnp.logical_not(has_lo))
    def _():
        from_lo[...] = jnp.zeros_like(from_lo)

    @pl.when(jnp.logical_not(has_hi))
    def _():
        from_hi[...] = jnp.zeros_like(from_hi)

    for g in range(2):
        arrived(from_lo.at[4 * g : 4 * g + 4], f_recv.at[0, g], has_lo)
        arrived(from_hi.at[4 * g : 4 * g + 4], f_recv.at[1, g], has_hi)
    build(0, lambda blk: from_lo[blk, 0])
    build(1, lambda blk: from_lo[blk, 1])
    build(4, lambda blk: from_hi[blk])
    acc[32:544, :] += product(0)
    acc[32:544, :] += product(1)
    acc[32:544, :] += product(4)

    def packed(at):
        rows = acc[at, :]
        left, right = rows[:, :128], rows[:, 128:]
        ln = iota((64, 128), 1)
        side = jnp.where(ln < 64, right[:64], pltpu.roll(right[64:], 64, 1))
        return jnp.concatenate([left, side], axis=0)

    @pl.loop(0, 8)
    def _(m):
        send2[m] = packed(pl.ds(pl.multiple_of(64 * m, 64), 128)).astype(BF16)

    for e, d in FAR + NEAR:
        m = peer(e, d)
        send(send2.at[m], recv2.at[n], s2_send.at[m], s2_recv.at[n], (w, m))
    forward(1)
    to_sibling(0)

    total = packed(pl.ds(pl.multiple_of(64 * n, 64), 128))
    for e, d in NEAR + FAR:
        m = peer(e, d)
        arrived(recv2.at[m], s2_recv.at[m])
        total = total + recv2[m].astype(F32)
    side = total[128:192]
    side = jnp.concatenate([side, pltpu.roll(side, 64, 1)], axis=0)
    conv = jnp.concatenate([total[:128], side[:, :64]], axis=1) + b1_ref[...]
    denom = beta_ref[...] + jnp.dot(
        conv * conv, gamma_ref[...], precision=lax.Precision.HIGHEST, preferred_element_type=F32
    )
    latent = (conv * lax.rsqrt(denom)).astype(BF16)
    lat_ref[...] = latent[32:96]

    k, l = iota((192, 256), 0), iota((192, 256), 1)
    spread = ((l & 31) < 24) & (k == 24 * (l >> 5) + (l & 31))
    spread = jnp.where(spread, 1.0, 0.0).astype(BF16)

    def spread_out(values, first):
        row = first + (iota((values.shape[0], 256), 0) >> 4)
        out = jnp.dot(values.astype(BF16), spread, preferred_element_type=F32)
        return jnp.where((row >= 0) & (row < 32), out, 0.0).astype(BF16)

    def exchange(buf, ssem, rsem):
        send(buf.at[1], buf.at[0], ssem.at[0], rsem.at[0], (hi, n), has_hi)
        send(buf.at[1], buf.at[2], ssem.at[1], rsem.at[1], (lo, n), has_lo)

    def layer_of(layer, buf, buf_q, rsem, rows):
        def shifts(z):
            x = buf[z].astype(F32)
            buf_q[z, 0] = rows_shifted(x, -1).astype(BF16)
            buf_q[z, 1] = rows_shifted(x, 1).astype(BF16)

        sums = [jnp.zeros((rows, 256), F32)] * 2

        def taps(z):
            for tap in range(9 * z, 9 * z + 9):
                _, b, c = TAPS[tap]
                at = pl.ds(16 * b, rows)
                left = buf[z, at, :] if c == 1 else buf_q[z, c // 2, at, :]
                kern = jnp.concatenate(
                    [wts[layer, 3 * (tap // 2) + tap % 2], wts[layer, 3 * (tap // 2) + 2]], axis=1
                )
                sums[tap % 2] += jnp.dot(left, kern, preferred_element_type=F32)

        shifts(1)
        taps(1)

        @pl.when(jnp.logical_not(has_lo))
        def _():
            buf[0] = jnp.zeros_like(buf[0])

        @pl.when(jnp.logical_not(has_hi))
        def _():
            buf[2] = jnp.zeros_like(buf[2])

        arrived(buf.at[0], rsem.at[0], has_lo)
        shifts(0)
        taps(0)
        arrived(buf.at[2], rsem.at[1], has_hi)
        shifts(2)
        taps(2)
        even, odd = sums
        side = even[:, 128:] + pltpu.roll(odd[:, 128:], 64, 1)
        return jnp.concatenate([even[:, :128] + odd[:, :128], side[:, :64]], axis=1)

    lat_p[1] = spread_out(jnp.abs(latent), 4 * n - 2)
    exchange(lat_p, l_send, l_recv)
    other = pl.ds(21 * (1 - core), 21)
    arrived(wts.at[0, other], c_recv.at[0])
    to_sibling(1)
    hidden = jnp.maximum(layer_of(0, lat_p, lat_q, l_recv, 96) + b2_ref[...], 0.0)
    hid_p[1] = spread_out(hidden, 4 * n - 1)
    exchange(hid_p, h_send, h_recv)
    arrived(wts.at[1, other], c_recv.at[1])
    s = layer_of(1, hid_p, hid_q, h_recv, 64) + b3_ref[...]
    sc_ref[...] = 0.11 + (jnp.maximum(s, 0.0) + jnp.log1p(jnp.exp(-jnp.abs(s))))

    for copy, when in sent:
        if when is None:
            copy.wait_send()
        else:
            pl.when(when)(copy.wait_send)


def on_device(density, w1, b1, beta, gamma, w2, b2, w3, b3):
    vmem = pl.BlockSpec(memory_space=pltpu.VMEM)
    dma = pltpu.SemaphoreType.DMA
    latent, scales = pl.pallas_call(
        kernel,
        out_shape=(
            jax.ShapeDtypeStruct((64, 192), BF16),
            jax.ShapeDtypeStruct((64, 192), F32),
        ),
        in_specs=[vmem] * 9,
        out_specs=(vmem, vmem),
        scratch_shapes=[
            pltpu.VMEM((8, 2, 64, 128), BF16),
            pltpu.VMEM((8, 2, 64, 128), BF16),
            pltpu.VMEM((8, 2, 64, 128), BF16),
            pltpu.VMEM((8, 64, 128), BF16),
            pltpu.VMEM((5, 544, 256), BF16),
            pltpu.VMEM((15, 256, 256), BF16),
            pltpu.VMEM((576, 256), F32),
            pltpu.VMEM((8, 192, 128), BF16),
            pltpu.VMEM((8, 192, 128), BF16),
            pltpu.VMEM((2, 42, 256, 128), BF16),
            pltpu.VMEM((3, 128, 256), BF16),
            pltpu.VMEM((3, 2, 128, 256), BF16),
            pltpu.VMEM((3, 96, 256), BF16),
            pltpu.VMEM((3, 2, 96, 256), BF16),
            dma((8,)), dma((8,)),
            dma((2, 2)), dma((2, 2)),
            dma((8,)), dma((8,)),
            dma((2, 7)), dma((2, 8)),
            dma((2,)), dma((2,)),
            dma((2,)), dma((2,)),
            dma((2,)), dma((2,)),
        ],
        compiler_params=pltpu.CompilerParams(
            collective_id=0, has_side_effects=True, vmem_limit_bytes=48 * 2**20
        ),
    )(
        density.reshape(512, 192),
        w1.reshape(25, 120, 192),
        b1.reshape(1, 192),
        beta.reshape(1, 192),
        gamma,
        w2.reshape(27, 24, 192),
        b2.reshape(1, 192),
        w3.reshape(27, 24, 192),
        b3.reshape(1, 192),
    )
    return latent.reshape(1, 4, 16, 192), scales.reshape(1, 4, 16, 192)


def solution(mesh):
    in_specs = (
        P("wide", "narrow", None, None),
        P(None, None, None, "narrow", None),
        P(),
        P(),
        P(),
        P(None, None, None, "narrow", None),
        P(),
        P(None, None, None, "narrow", None),
        P(),
    )
    out_specs = (P("wide", "narrow", None, None), P("wide", "narrow", None, None))
    return jax.shard_map(
        on_device, mesh=mesh, in_specs=in_specs, out_specs=out_specs, check_vma=False
    )
```

```python
import jax
import jax.numpy as jnp
from jax import lax
from jax.experimental import pallas as pl
from jax.experimental.pallas import tpu as pltpu
from jax.sharding import PartitionSpec as P

MESH = pl.DeviceIdType.MESH
F32 = jnp.float32
BF16 = jnp.bfloat16

FAR = ((1, 2), (1, 1), (1, 3), (1, 0))
NEAR = ((0, 2), (0, 1), (0, 3))
TAPS = tuple((a, b, c) for a in range(3) for b in range(3) for c in range(3))


def iota(shape, dim):
    return lax.broadcasted_iota(jnp.int32, shape, dim)


def rows_shifted(x, by):
    n = x.shape[0]
    col = iota(x.shape, 0) & 15
    if by == -1:
        return jnp.where(col == 0, 0.0, pltpu.roll(x, 1, 0))
    return jnp.where(col == 15, 0.0, pltpu.roll(x, n - 1, 0))


def kernel(
    x_in, w1_in, b1_in, beta_in, gamma_in, w2_in, b2_in, w3_in, b3_in,
    lat_ref, sc_ref,
    x_ref, w1_ref, b1_ref, beta_ref, gamma_ref, w2_ref, b2_ref, w3_ref, b3_ref, in_sem,
    send1, recv1, from_lo, from_hi, planes, w1k, acc, send2, recv2, wts,
    lat_p, lat_q, hid_p, hid_q,
    s1_send, s1_recv, f_send, f_recv, s2_send, s2_recv,
    g_send, g_recv, c_send, c_recv, l_send, l_recv, h_send, h_recv,
):
    loads = [
        pltpu.make_async_copy(src, dst, in_sem.at[i])
        for i, (src, dst) in enumerate((
            (x_in, x_ref), (w2_in, w2_ref), (w3_in, w3_ref), (w1_in, w1_ref), (gamma_in, gamma_ref),
            (b1_in, b1_ref), (beta_in, beta_ref), (b2_in, b2_ref), (b3_in, b3_ref),
        ))
    ]
    for load in loads:
        load.start()
    w, n = lax.axis_index("wide"), lax.axis_index("narrow")
    wide = lax.axis_size("wide")
    zh, xx, core = n // 4, n % 4, w % 2
    has_lo, has_hi = w > 0, w < wide - 1
    lo, hi = jnp.maximum(w - 1, 0), jnp.minimum(w + 1, wide - 1)
    sibling = w + 1 - 2 * core

    def peer(e, d):
        return ((zh + e) % 2) * 4 + (xx + d) % 4

    sent = []

    def send(src, dst, ssem, rsem, device, when=None):
        copy = pltpu.make_async_remote_copy(
            src_ref=src, dst_ref=dst, send_sem=ssem, recv_sem=rsem,
            device_id=device, device_id_type=MESH,
        )
        if when is None:
            copy.start()
        else:
            pl.when(when)(copy.start)
        sent.append((copy, when))

    def arrived(dst, rsem, when=None):
        copy = pltpu.make_async_remote_copy(
            src_ref=dst, dst_ref=dst, send_sem=rsem, recv_sem=rsem,
            device_id=(sibling, n), device_id_type=MESH,
        )
        if when is None:
            copy.wait_recv()
        else:
            pl.when(when)(copy.wait_recv)

    barrier = pltpu.get_barrier_semaphore()
    for e, d in FAR + NEAR:
        pl.semaphore_signal(barrier, inc=1, device_id=(w, peer(e, d)), device_id_type=MESH)

    @pl.when(has_lo)
    def _():
        pl.semaphore_signal(barrier, inc=1, device_id=(lo, n), device_id_type=MESH)

    @pl.when(has_hi)
    def _():
        pl.semaphore_signal(barrier, inc=1, device_id=(hi, n), device_id_type=MESH)

    loads[0].wait()
    i, j = iota((256, 256), 0), iota((256, 256), 1)
    source = ((i >> 4) & 3) * 64 + (i >> 7) * 32 + (i & 15) * 2 + ((i >> 6) & 1)
    perm = jnp.where(j == source, 1.0, 0.0).astype(BF16)
    cut = [
        jnp.dot(perm, x_ref[256 * z : 256 * z + 256, :], preferred_element_type=F32).astype(BF16)
        for z in range(2)
    ]
    parts = [
        jnp.concatenate([cut[z][64 * t : 64 * t + 64] for z in range(2)], axis=0) for t in range(4)
    ]
    k, l = iota((192, 256), 0), iota((192, 256), 1)
    lane, which = l & 127, l >> 7
    for pair in range(4):
        total = jnp.zeros((128, 256), F32)
        for t in range(4):
            inside = (lane >= 24 * t) & (lane < 24 * t + 24)
            pick = inside & (k == 24 * (2 * pair + which) + lane - 24 * t)
            pick = jnp.where(pick, 1.0, 0.0).astype(BF16)
            total = total + jnp.dot(parts[t], pick, preferred_element_type=F32)
        total = total.astype(BF16)
        for side in range(2):
            for z in range(2):
                send1[2 * pair + side, z] = total[64 * z : 64 * z + 64, 128 * side : 128 * side + 128]

    pl.semaphore_wait(barrier, 7 + has_lo.astype(jnp.int32) + has_hi.astype(jnp.int32))

    for e, d in FAR + NEAR:
        m = peer(e, d)
        send(send1.at[m], recv1.at[n], s1_send.at[m], s1_recv.at[n], (w, m))
    recv1[n] = send1[n]

    for load in loads[1:]:
        load.wait()

    for layer, ref in ((0, w2_ref), (1, w3_ref)):

        @pl.loop(0, 7)
        def _(t, layer=layer, ref=ref):
            tap = 14 * core + 2 * t
            even = ref[tap].astype(F32)
            odd = ref[jnp.minimum(tap + 1, 26)].astype(F32)
            odd = jnp.where(tap + 1 < 27, odd, 0.0)
            at = 21 * core + 3 * t
            wts[layer, at, n] = even[:, :128].astype(BF16)
            wts[layer, at + 1, n] = odd[:, :128].astype(BF16)
            both = jnp.concatenate([even[:, 128:], odd[:, 128:]], axis=1)
            wts[layer, at + 2, n] = both.astype(BF16)

    half = pl.ds(21 * core, 21)

    def slice_of(layer, m):
        return wts.at[layer, half, m]

    mirror = peer(1, 0)

    def to_peers(layer):
        part = slice_of(layer, n)
        for at, (e, d) in enumerate(((1, 0),) + NEAR):
            send(part, part, g_send.at[layer, at], g_recv.at[layer, n], (w, peer(e, d)))

    def forward(layer):
        part = slice_of(layer, mirror)
        arrived(part, g_recv.at[layer, mirror])
        for at, (e, d) in enumerate(NEAR):
            send(part, part, g_send.at[layer, 4 + at], g_recv.at[layer, mirror], (w, peer(e, d)))

    def to_sibling(layer):
        for e, d in NEAR + FAR[:3]:
            m = peer(e, d)
            arrived(slice_of(layer, m), g_recv.at[layer, m])
        part = wts.at[layer, half]
        send(part, part, c_send.at[layer], c_recv.at[layer], (sibling, n))

    to_peers(0)

    w1k[...] = jnp.zeros_like(w1k)

    @pl.loop(0, 5)
    def _(a):
        for b in range(5):
            step, rp = b // 2, b % 2
            at = a * 3 + step
            v = w1_ref[a * 5 + b].astype(F32)
            last = jnp.concatenate([v[96:120], jnp.zeros((8, 192), F32)], axis=0)
            w1k[at, 48 * rp : 48 * rp + 48, 0:192] = v[0:48].astype(BF16)
            w1k[at, 128 + 48 * rp : 176 + 48 * rp, 0:192] = v[48:96].astype(BF16)
            w1k[at, 96 + 128 * rp : 128 + 128 * rp, 0:192] = last.astype(BF16)

    planes[:, 0:16, :] = jnp.zeros((5, 16, 256), BF16)
    planes[:, 528:544, :] = jnp.zeros((5, 16, 256), BF16)
    acc[0:32, :] = jnp.zeros((32, 256), F32)
    acc[544:576, :] = jnp.zeros((32, 256), F32)

    for turn in range(2):
        for e, d in NEAR if turn == 0 else FAR:
            m = peer(e, d)
            arrived(recv1.at[m], s1_recv.at[m])
        g = (zh + turn) % 2
        four = pl.ds(4 * g, 4)
        send(recv1.at[four], from_lo.at[four], f_send.at[0, turn], f_recv.at[0, g], (hi, n), has_hi)
        send(
            recv1.at[four, 0], from_hi.at[four], f_send.at[1, turn], f_recv.at[1, g], (lo, n), has_lo
        )
        if turn == 0:
            to_peers(1)

    def build(a, read, begin=0, count=8):
        @pl.loop(0, count)
        def _(step):
            blk = begin + step
            x = read(blk).astype(F32)
            ln = iota(x.shape, 1)
            after = rows_shifted(x, 1)
            before = jnp.where(ln < 96, rows_shifted(x, -1), pltpu.roll(after, 96, 1))
            same = jnp.where(ln < 96, x, pltpu.roll(after, 48, 1))
            at = pl.ds(pl.multiple_of(16 + 64 * blk, 16), 64)
            planes[a, at, 0:128] = before.astype(BF16)
            planes[a, at, 128:256] = same.astype(BF16)

    def product(a, first=0, size=512):
        rows = jnp.concatenate(
            [planes[a, pl.ds(first + 16 * s, size), :] for s in range(3)], axis=1
        )
        return jnp.dot(
            rows, w1k[3 * a : 3 * a + 3].reshape(768, 256), preferred_element_type=F32
        )

    build(2, lambda blk: recv1[blk, 0])
    build(3, lambda blk: recv1[blk, 1])
    acc[32:544, :] = product(2) + product(3)

    @pl.when(jnp.logical_not(has_lo))
    def _():
        from_lo[...] = jnp.zeros_like(from_lo)

    @pl.when(jnp.logical_not(has_hi))
    def _():
        from_hi[...] = jnp.zeros_like(from_hi)

    for turn in range(2):
        g = (zh + turn) % 2
        four = pl.ds(4 * g, 4)
        arrived(from_lo.at[four], f_recv.at[0, g], has_lo)
        arrived(from_hi.at[four], f_recv.at[1, g], has_hi)
        if turn == 1:
            forward(0)
        build(0, lambda blk: from_lo[blk, 0], 4 * g, 4)
        build(1, lambda blk: from_lo[blk, 1], 4 * g, 4)
        build(4, lambda blk: from_hi[blk], 4 * g, 4)
        size = (240, 272)[turn]
        first = pl.multiple_of(zh * 272 if turn == 0 else (1 - zh) * 240, 16)
        add = product(0, first, size) + product(1, first, size) + product(4, first, size)
        acc[pl.ds(pl.multiple_of(32 + first, 16), size), :] += add

    def packed(at):
        rows = acc[at, :]
        left, right = rows[:, :128], rows[:, 128:]
        ln = iota((64, 128), 1)
        side = jnp.where(ln < 64, right[:64], pltpu.roll(right[64:], 64, 1))
        return jnp.concatenate([left, side], axis=0)

    @pl.loop(0, 8)
    def _(m):
        send2[m] = packed(pl.ds(pl.multiple_of(64 * m, 64), 128)).astype(BF16)

    for e, d in FAR + NEAR:
        m = peer(e, d)
        send(send2.at[m], recv2.at[n], s2_send.at[m], s2_recv.at[n], (w, m))
    forward(1)
    to_sibling(0)

    total = packed(pl.ds(pl.multiple_of(64 * n, 64), 128))
    for e, d in NEAR + FAR:
        m = peer(e, d)
        arrived(recv2.at[m], s2_recv.at[m])
        total = total + recv2[m].astype(F32)
    side = total[128:192]
    side = jnp.concatenate([side, pltpu.roll(side, 64, 1)], axis=0)
    conv = jnp.concatenate([total[:128], side[:, :64]], axis=1) + b1_ref[...]
    denom = beta_ref[...] + jnp.dot(
        conv * conv, gamma_ref[...], precision=lax.Precision.HIGHEST, preferred_element_type=F32
    )
    latent = (conv * lax.rsqrt(denom)).astype(BF16)
    lat_ref[...] = latent[32:96]

    def inside(values, first):
        row = first + (iota(values.shape, 0) >> 4)
        return jnp.where((row >= 0) & (row < 32), values, 0.0).astype(BF16)

    def exchange(buf, ssem, rsem):
        send(buf.at[1], buf.at[0], ssem.at[0], rsem.at[0], (hi, n), has_hi)
        send(buf.at[1], buf.at[2], ssem.at[1], rsem.at[1], (lo, n), has_lo)

    def kernel_of(layer, at):
        return wts[layer, at].reshape(192, 128)

    def layer_of(layer, buf, buf_q, rsem, rows):
        def shifts(z):
            x = buf[z].astype(F32)
            buf_q[z, 0] = rows_shifted(x, -1).astype(BF16)
            buf_q[z, 1] = rows_shifted(x, 1).astype(BF16)

        sums = [jnp.zeros((rows, 256), F32)] * 2

        def taps(z):
            for tap in range(9 * z, 9 * z + 9):
                _, b, c = TAPS[tap]
                at = pl.ds(16 * b, rows)
                left = buf[z, at, :] if c == 1 else buf_q[z, c // 2, at, :]
                kern = jnp.concatenate(
                    [kernel_of(layer, 3 * (tap // 2) + tap % 2), kernel_of(layer, 3 * (tap // 2) + 2)],
                    axis=1,
                )
                sums[tap % 2] += jnp.dot(left, kern, preferred_element_type=F32)

        shifts(1)
        taps(1)

        @pl.when(jnp.logical_not(has_lo))
        def _():
            buf[0] = jnp.zeros_like(buf[0])

        @pl.when(jnp.logical_not(has_hi))
        def _():
            buf[2] = jnp.zeros_like(buf[2])

        arrived(buf.at[0], rsem.at[0], has_lo)
        shifts(0)
        taps(0)
        arrived(buf.at[2], rsem.at[1], has_hi)
        shifts(2)
        taps(2)
        even, odd = sums
        side = even[:, 128:] + pltpu.roll(odd[:, 128:], 64, 1)
        return jnp.concatenate([even[:, :128] + odd[:, :128], side[:, :64]], axis=1)

    lat_p[1] = inside(jnp.abs(latent.astype(F32)), 4 * n - 2)
    exchange(lat_p, l_send, l_recv)
    other = pl.ds(21 * (1 - core), 21)
    arrived(wts.at[0, other], c_recv.at[0])
    to_sibling(1)
    hidden = jnp.maximum(layer_of(0, lat_p, lat_q, l_recv, 96) + b2_ref[...], 0.0)
    hid_p[1] = inside(hidden, 4 * n - 1)
    exchange(hid_p, h_send, h_recv)
    arrived(wts.at[1, other], c_recv.at[1])
    s = layer_of(1, hid_p, hid_q, h_recv, 64) + b3_ref[...]
    sc_ref[...] = 0.11 + (jnp.maximum(s, 0.0) + jnp.log1p(jnp.exp(-jnp.abs(s))))

    for copy, when in sent:
        if when is None:
            copy.wait_send()
        else:
            pl.when(when)(copy.wait_send)


def on_device(density, w1, b1, beta, gamma, w2, b2, w3, b3):
    vmem = pl.BlockSpec(memory_space=pltpu.VMEM)
    dma = pltpu.SemaphoreType.DMA
    latent, scales = pl.pallas_call(
        kernel,
        out_shape=(
            jax.ShapeDtypeStruct((64, 192), BF16),
            jax.ShapeDtypeStruct((64, 192), F32),
        ),
        in_specs=[pl.BlockSpec(memory_space=pl.ANY)] * 9,
        out_specs=(vmem, vmem),
        scratch_shapes=[
            pltpu.VMEM((512, 192), BF16),
            pltpu.VMEM((25, 120, 192), BF16),
            pltpu.VMEM((1, 192), F32),
            pltpu.VMEM((1, 192), F32),
            pltpu.VMEM((192, 192), F32),
            pltpu.VMEM((27, 24, 192), BF16),
            pltpu.VMEM((1, 192), F32),
            pltpu.VMEM((27, 24, 192), BF16),
            pltpu.VMEM((1, 192), F32),
            dma((9,)),
            pltpu.VMEM((8, 2, 64, 128), BF16),
            pltpu.VMEM((8, 2, 64, 128), BF16),
            pltpu.VMEM((8, 2, 64, 128), BF16),
            pltpu.VMEM((8, 64, 128), BF16),
            pltpu.VMEM((5, 544, 256), BF16),
            pltpu.VMEM((15, 256, 256), BF16),
            pltpu.VMEM((576, 256), F32),
            pltpu.VMEM((8, 192, 128), BF16),
            pltpu.VMEM((8, 192, 128), BF16),
            pltpu.VMEM((2, 42, 8, 24, 128), BF16),
            pltpu.VMEM((3, 128, 192), BF16),
            pltpu.VMEM((3, 2, 128, 192), BF16),
            pltpu.VMEM((3, 96, 192), BF16),
            pltpu.VMEM((3, 2, 96, 192), BF16),
            dma((8,)), dma((8,)),
            dma((2, 2)), dma((2, 2)),
            dma((8,)), dma((8,)),
            dma((2, 7)), dma((2, 8)),
            dma((2,)), dma((2,)),
            dma((2,)), dma((2,)),
            dma((2,)), dma((2,)),
        ],
        compiler_params=pltpu.CompilerParams(
            collective_id=0, has_side_effects=True, vmem_limit_bytes=60 * 2**20
        ),
    )(
        density.reshape(512, 192),
        w1.reshape(25, 120, 192),
        b1.reshape(1, 192),
        beta.reshape(1, 192),
        gamma,
        w2.reshape(27, 24, 192),
        b2.reshape(1, 192),
        w3.reshape(27, 24, 192),
        b3.reshape(1, 192),
    )
    return latent.reshape(1, 4, 16, 192), scales.reshape(1, 4, 16, 192)


def solution(mesh):
    in_specs = (
        P("wide", "narrow", None, None),
        P(None, None, None, "narrow", None),
        P(),
        P(),
        P(),
        P(None, None, None, "narrow", None),
        P(),
        P(None, None, None, "narrow", None),
        P(),
    )
    out_specs = (P("wide", "narrow", None, None), P("wide", "narrow", None, None))
    return jax.shard_map(
        on_device, mesh=mesh, in_specs=in_specs, out_specs=out_specs, check_vma=False
    )
```

```python
import jax
import jax.numpy as jnp
from jax import lax
from jax.experimental import pallas as pl
from jax.experimental.pallas import tpu as pltpu
from jax.sharding import PartitionSpec as P

MESH = pl.DeviceIdType.MESH
F32 = jnp.float32
BF16 = jnp.bfloat16

FAR = ((1, 2), (1, 1), (1, 3), (1, 0))
NEAR = ((0, 2), (0, 1), (0, 3))
TAPS = tuple((a, b, c) for a in range(3) for b in range(3) for c in range(3))


def iota(shape, dim):
    return lax.broadcasted_iota(jnp.int32, shape, dim)


def rows_shifted(x, by):
    n = x.shape[0]
    col = iota(x.shape, 0) & 15
    if by == -1:
        return jnp.where(col == 0, 0.0, pltpu.roll(x, 1, 0))
    return jnp.where(col == 15, 0.0, pltpu.roll(x, n - 1, 0))


def kernel(
    x_in, w1_in, b1_in, beta_in, gamma_in, w2_in, b2_in, w3_in, b3_in,
    lat_ref, sc_ref,
    x_ref, w1_ref, b1_ref, beta_ref, gamma_ref, w2_ref, b2_ref, w3_ref, b3_ref, in_sem,
    send1, recv1, from_lo, from_hi, planes, w1k, acc, send2, recv2, wts,
    lat_p, lat_q, hid_p, hid_q,
    s1_send, s1_recv, f_send, f_recv, s2_send, s2_recv,
    g_send, g_recv, y_send, y_recv, c_send, c_recv, l_send, l_recv, h_send, h_recv,
):
    loads = [
        pltpu.make_async_copy(src, dst, in_sem.at[i])
        for i, (src, dst) in enumerate((
            (x_in, x_ref), (w2_in, w2_ref), (w3_in, w3_ref), (w1_in, w1_ref), (gamma_in, gamma_ref),
            (b1_in, b1_ref), (beta_in, beta_ref), (b2_in, b2_ref), (b3_in, b3_ref),
        ))
    ]
    for load in loads:
        load.start()
    w, n = lax.axis_index("wide"), lax.axis_index("narrow")
    wide = lax.axis_size("wide")
    zh, xx, core = n // 4, n % 4, w % 2
    yy = (w // 2) % 8
    y_up, y_down = w + 2 * ((yy + 1) % 8 - yy), w + 2 * ((yy + 7) % 8 - yy)
    quarter = 2 * core + yy % 2
    has_lo, has_hi = w > 0, w < wide - 1
    lo, hi = jnp.maximum(w - 1, 0), jnp.minimum(w + 1, wide - 1)
    sibling = w + 1 - 2 * core

    def peer(e, d):
        return ((zh + e) % 2) * 4 + (xx + d) % 4

    sent = []

    def send(src, dst, ssem, rsem, device, when=None):
        copy = pltpu.make_async_remote_copy(
            src_ref=src, dst_ref=dst, send_sem=ssem, recv_sem=rsem,
            device_id=device, device_id_type=MESH,
        )
        if when is None:
            copy.start()
        else:
            pl.when(when)(copy.start)
        sent.append((copy, when))

    def arrived(dst, rsem, when=None):
        copy = pltpu.make_async_remote_copy(
            src_ref=dst, dst_ref=dst, send_sem=rsem, recv_sem=rsem,
            device_id=(sibling, n), device_id_type=MESH,
        )
        if when is None:
            copy.wait_recv()
        else:
            pl.when(when)(copy.wait_recv)

    barrier = pltpu.get_barrier_semaphore()
    for e, d in FAR + NEAR:
        pl.semaphore_signal(barrier, inc=1, device_id=(w, peer(e, d)), device_id_type=MESH)

    for y in (y_up, y_down):
        pl.semaphore_signal(barrier, inc=1, device_id=(y, n), device_id_type=MESH)

    @pl.when(has_lo)
    def _():
        pl.semaphore_signal(barrier, inc=1, device_id=(lo, n), device_id_type=MESH)

    @pl.when(has_hi)
    def _():
        pl.semaphore_signal(barrier, inc=1, device_id=(hi, n), device_id_type=MESH)

    loads[0].wait()
    i, j = iota((256, 256), 0), iota((256, 256), 1)
    source = ((i >> 4) & 3) * 64 + (i >> 7) * 32 + (i & 15) * 2 + ((i >> 6) & 1)
    perm = jnp.where(j == source, 1.0, 0.0).astype(BF16)
    cut = [
        jnp.dot(perm, x_ref[256 * z : 256 * z + 256, :], preferred_element_type=F32).astype(BF16)
        for z in range(2)
    ]
    parts = [
        jnp.concatenate([cut[z][64 * t : 64 * t + 64] for z in range(2)], axis=0) for t in range(4)
    ]
    k, l = iota((192, 256), 0), iota((192, 256), 1)
    lane, which = l & 127, l >> 7
    for pair in range(4):
        total = jnp.zeros((128, 256), F32)
        for t in range(4):
            inside = (lane >= 24 * t) & (lane < 24 * t + 24)
            pick = inside & (k == 24 * (2 * pair + which) + lane - 24 * t)
            pick = jnp.where(pick, 1.0, 0.0).astype(BF16)
            total = total + jnp.dot(parts[t], pick, preferred_element_type=F32)
        for side in range(2):
            first = total[:64, 128 * side : 128 * side + 128]
            second = pltpu.roll(total[64:, 128 * side : 128 * side + 128], 96, 1)
            ln = iota((64, 128), 1)
            rest = jnp.where(ln[:32] < 64, second[:32], pltpu.roll(second[32:], 64, 1))
            block = jnp.concatenate([jnp.where(ln < 96, first, second), rest], axis=0)
            send1[2 * pair + side] = block.astype(BF16)

    pl.semaphore_wait(barrier, 9 + has_lo.astype(jnp.int32) + has_hi.astype(jnp.int32))

    for e, d in FAR + NEAR:
        m = peer(e, d)
        send(send1.at[m], recv1.at[n], s1_send.at[m], s1_recv.at[n], (w, m))
    recv1[n] = send1[n]

    for load in loads[1:]:
        load.wait()

    for layer, ref in ((0, w2_ref), (1, w3_ref)):

        @pl.loop(0, 11)
        def _(t, layer=layer, ref=ref):
            at = 11 * quarter + t
            tap, kind = 2 * (at // 3), at % 3
            even = ref[jnp.minimum(tap, 26)].astype(F32)
            odd = ref[jnp.minimum(tap + 1, 26)].astype(F32)
            odd = jnp.where(tap + 1 < 27, odd, 0.0)
            both = jnp.concatenate([even[:, 128:], odd[:, 128:]], axis=1)
            value = jnp.where(kind == 0, even[:, :128], jnp.where(kind == 1, odd[:, :128], both))
            wts[layer, at, n] = value.astype(BF16)

    mirror = peer(1, 0)

    def slice_of(layer, m):
        return wts.at[layer, pl.ds(11 * quarter, 11), m]

    def to_peers(layer):
        part = slice_of(layer, n)
        for at, (e, d) in enumerate(((1, 0),) + NEAR):
            send(part, part, g_send.at[layer, at], g_recv.at[layer, n], (w, peer(e, d)))

    def forward(layer):
        part = slice_of(layer, mirror)
        arrived(part, g_recv.at[layer, mirror])
        for at, (e, d) in enumerate(NEAR):
            send(part, part, g_send.at[layer, 4 + at], g_recv.at[layer, mirror], (w, peer(e, d)))

    def y_part(layer, q, up, half):
        return wts.at[layer, pl.ds(11 * q + (0 if up else 6), 6 if up else 5), pl.ds(4 * half, 4)]

    def along_y(layer, turn):
        for e, d in NEAR if turn == 0 else FAR[:3]:
            m = peer(e, d)
            arrived(slice_of(layer, m), g_recv.at[layer, m])
        half = (zh + turn) % 2
        for up, y in ((1, y_up), (0, y_down)):
            part = y_part(layer, quarter, up, half)
            send(part, part, y_send.at[layer, turn, up], y_recv.at[layer, turn, up], (y, n))

    def to_sibling(layer):
        for turn in range(2):
            for up in (1, 0):
                part = y_part(layer, quarter + 1 - 2 * (yy % 2), up, (zh + turn) % 2)
                arrived(part, y_recv.at[layer, turn, up])
        part = wts.at[layer, pl.ds(22 * core, 22)]
        send(part, part, c_send.at[layer], c_recv.at[layer], (sibling, n))

    to_peers(0)

    w1k[...] = jnp.zeros_like(w1k)

    def fill(a, odd):
        for b in range(5):
            step, rp = b // 2, b % 2
            at = a * 3 + step
            v = w1_ref[a * 5 + b].astype(F32)
            last = jnp.concatenate([v[96:120], jnp.zeros((8, 192), F32)], axis=0)
            for base, rows in ((0, v[0:48]), (128, v[48:96])):
                rows = rows.astype(BF16)
                if not odd:
                    w1k[at, base + 48 * rp : base + 48 * rp + 48, 0:192] = rows
                elif rp == 0:
                    w1k[at, base + 96 : base + 128, 0:192] = rows[0:32]
                    w1k[at, base : base + 16, 0:192] = rows[32:48]
                else:
                    w1k[at, base + 16 : base + 64, 0:192] = rows
            gap = 128 * rp + (64 if odd else 96)
            w1k[at, gap : gap + 32, 0:192] = last.astype(BF16)

    @pl.loop(0, 3)
    def _(t):
        fill(2 * t, False)

    @pl.loop(0, 2)
    def _(t):
        fill(2 * t + 1, True)

    planes[:, 0:16, :] = jnp.zeros((5, 16, 256), BF16)
    planes[:, 528:544, :] = jnp.zeros((5, 16, 256), BF16)
    acc[0:32, :] = jnp.zeros((32, 256), F32)
    acc[544:576, :] = jnp.zeros((32, 256), F32)

    for turn in range(2):
        for e, d in NEAR if turn == 0 else FAR:
            m = peer(e, d)
            arrived(recv1.at[m], s1_recv.at[m])
        g = (zh + turn) % 2
        four = pl.ds(4 * g, 4)
        send(recv1.at[four], from_lo.at[four], f_send.at[0, turn], f_recv.at[0, g], (hi, n), has_hi)
        send(
            recv1.at[four, 0:64], from_hi.at[four], f_send.at[1, turn], f_recv.at[1, g], (lo, n), has_lo
        )
        if turn == 0:
            to_peers(1)

    def build(a, read, begin=0, count=8):
        @pl.loop(0, count)
        def _(step):
            blk = begin + step
            x = read(blk).astype(F32)
            ln = iota((64, 128), 1)
            kept = ln < 96
            if a % 2:
                rest = jnp.concatenate([x[64:], pltpu.roll(x[64:], 64, 1)], axis=0)
                x = jnp.where(kept, rest, x[:64])
                kept = (ln < 64) | (ln >= 96)
            after = rows_shifted(x, 1)
            before = jnp.where(kept, rows_shifted(x, -1), pltpu.roll(after, 96, 1))
            same = jnp.where(kept, x, pltpu.roll(after, 48, 1))
            at = pl.ds(pl.multiple_of(16 + 64 * blk, 16), 64)
            planes[a, at, 0:128] = before.astype(BF16)
            planes[a, at, 128:256] = same.astype(BF16)

    def product(a, first=0, size=512):
        rows = jnp.concatenate(
            [planes[a, pl.ds(first + 16 * s, size), :] for s in range(3)], axis=1
        )
        return jnp.dot(
            rows, w1k[3 * a : 3 * a + 3].reshape(768, 256), preferred_element_type=F32
        )

    along_y(0, 0)
    build(2, lambda blk: recv1[blk, 0:64])
    build(3, lambda blk: recv1[blk])
    acc[32:544, :] = product(2) + product(3)

    @pl.when(jnp.logical_not(has_lo))
    def _():
        from_lo[...] = jnp.zeros_like(from_lo)

    @pl.when(jnp.logical_not(has_hi))
    def _():
        from_hi[...] = jnp.zeros_like(from_hi)

    for turn in range(2):
        g = (zh + turn) % 2
        four = pl.ds(4 * g, 4)
        arrived(from_lo.at[four], f_recv.at[0, g], has_lo)
        arrived(from_hi.at[four], f_recv.at[1, g], has_hi)
        if turn == 0:
            forward(0)
        else:
            forward(1)
            along_y(1, 0)
        build(0, lambda blk: from_lo[blk, 0:64], 4 * g, 4)
        build(1, lambda blk: from_lo[blk], 4 * g, 4)
        build(4, lambda blk: from_hi[blk], 4 * g, 4)
        size = (240, 272)[turn]
        first = pl.multiple_of(zh * 272 if turn == 0 else (1 - zh) * 240, 16)
        add = product(0, first, size) + product(1, first, size) + product(4, first, size)
        acc[pl.ds(pl.multiple_of(32 + first, 16), size), :] += add

    def packed(at):
        rows = acc[at, :]
        left, right = rows[:, :128], rows[:, 128:]
        ln = iota((64, 128), 1)
        side = jnp.where(ln < 64, right[:64], pltpu.roll(right[64:], 64, 1))
        return jnp.concatenate([left, side], axis=0)

    @pl.loop(0, 8)
    def _(m):
        send2[m] = packed(pl.ds(pl.multiple_of(64 * m, 64), 128)).astype(BF16)

    for e, d in FAR + NEAR:
        m = peer(e, d)
        send(send2.at[m], recv2.at[n], s2_send.at[m], s2_recv.at[n], (w, m))
    along_y(0, 1)
    along_y(1, 1)
    to_sibling(0)

    total = packed(pl.ds(pl.multiple_of(64 * n, 64), 128))
    for e, d in NEAR + FAR:
        m = peer(e, d)
        arrived(recv2.at[m], s2_recv.at[m])
        total = total + recv2[m].astype(F32)
    side = total[128:192]
    side = jnp.concatenate([side, pltpu.roll(side, 64, 1)], axis=0)
    conv = jnp.concatenate([total[:128], side[:, :64]], axis=1) + b1_ref[...]
    denom = beta_ref[...] + jnp.dot(
        conv * conv, gamma_ref[...], precision=lax.Precision.HIGHEST, preferred_element_type=F32
    )
    latent = (conv * lax.rsqrt(denom)).astype(BF16)
    lat_ref[...] = latent[32:96]

    def inside(values, first):
        row = first + (iota(values.shape, 0) >> 4)
        return jnp.where((row >= 0) & (row < 32), values, 0.0).astype(BF16)

    def exchange(buf, ssem, rsem):
        send(buf.at[1], buf.at[0], ssem.at[0], rsem.at[0], (hi, n), has_hi)
        send(buf.at[1], buf.at[2], ssem.at[1], rsem.at[1], (lo, n), has_lo)

    def kernel_of(layer, at):
        return wts[layer, at].reshape(192, 128)

    def layer_of(layer, buf, buf_q, rsem, rows):
        def shifts(z):
            x = buf[z].astype(F32)
            buf_q[z, 0] = rows_shifted(x, -1).astype(BF16)
            buf_q[z, 1] = rows_shifted(x, 1).astype(BF16)

        sums = [jnp.zeros((rows, 256), F32)] * 2

        def taps(z):
            for tap in range(9 * z, 9 * z + 9):
                _, b, c = TAPS[tap]
                at = pl.ds(16 * b, rows)
                left = buf[z, at, :] if c == 1 else buf_q[z, c // 2, at, :]
                kern = jnp.concatenate(
                    [kernel_of(layer, 3 * (tap // 2) + tap % 2), kernel_of(layer, 3 * (tap // 2) + 2)],
                    axis=1,
                )
                sums[tap % 2] += jnp.dot(left, kern, preferred_element_type=F32)

        shifts(1)
        taps(1)

        @pl.when(jnp.logical_not(has_lo))
        def _():
            buf[0] = jnp.zeros_like(buf[0])

        @pl.when(jnp.logical_not(has_hi))
        def _():
            buf[2] = jnp.zeros_like(buf[2])

        arrived(buf.at[0], rsem.at[0], has_lo)
        shifts(0)
        taps(0)
        arrived(buf.at[2], rsem.at[1], has_hi)
        shifts(2)
        taps(2)
        even, odd = sums
        side = even[:, 128:] + pltpu.roll(odd[:, 128:], 64, 1)
        return jnp.concatenate([even[:, :128] + odd[:, :128], side[:, :64]], axis=1)

    lat_p[1] = inside(jnp.abs(latent.astype(F32)), 4 * n - 2)
    exchange(lat_p, l_send, l_recv)
    other = pl.ds(22 * (1 - core), 22)
    arrived(wts.at[0, other], c_recv.at[0])
    to_sibling(1)
    hidden = jnp.maximum(layer_of(0, lat_p, lat_q, l_recv, 96) + b2_ref[...], 0.0)
    hid_p[1] = inside(hidden, 4 * n - 1)
    exchange(hid_p, h_send, h_recv)
    arrived(wts.at[1, other], c_recv.at[1])
    s = layer_of(1, hid_p, hid_q, h_recv, 64) + b3_ref[...]
    sc_ref[...] = 0.11 + (jnp.maximum(s, 0.0) + jnp.log1p(jnp.exp(-jnp.abs(s))))

    for copy, when in sent:
        if when is None:
            copy.wait_send()
        else:
            pl.when(when)(copy.wait_send)


def on_device(density, w1, b1, beta, gamma, w2, b2, w3, b3):
    vmem = pl.BlockSpec(memory_space=pltpu.VMEM)
    dma = pltpu.SemaphoreType.DMA
    latent, scales = pl.pallas_call(
        kernel,
        out_shape=(
            jax.ShapeDtypeStruct((64, 192), BF16),
            jax.ShapeDtypeStruct((64, 192), F32),
        ),
        in_specs=[pl.BlockSpec(memory_space=pl.ANY)] * 9,
        out_specs=(vmem, vmem),
        scratch_shapes=[
            pltpu.VMEM((512, 192), BF16),
            pltpu.VMEM((25, 120, 192), BF16),
            pltpu.VMEM((1, 192), F32),
            pltpu.VMEM((1, 192), F32),
            pltpu.VMEM((192, 192), F32),
            pltpu.VMEM((27, 24, 192), BF16),
            pltpu.VMEM((1, 192), F32),
            pltpu.VMEM((27, 24, 192), BF16),
            pltpu.VMEM((1, 192), F32),
            dma((9,)),
            pltpu.VMEM((8, 96, 128), BF16),
            pltpu.VMEM((8, 96, 128), BF16),
            pltpu.VMEM((8, 96, 128), BF16),
            pltpu.VMEM((8, 64, 128), BF16),
            pltpu.VMEM((5, 544, 256), BF16),
            pltpu.VMEM((15, 256, 256), BF16),
            pltpu.VMEM((576, 256), F32),
            pltpu.VMEM((8, 192, 128), BF16),
            pltpu.VMEM((8, 192, 128), BF16),
            pltpu.VMEM((2, 44, 8, 24, 128), BF16),
            pltpu.VMEM((3, 128, 192), BF16),
            pltpu.VMEM((3, 2, 128, 192), BF16),
            pltpu.VMEM((3, 96, 192), BF16),
            pltpu.VMEM((3, 2, 96, 192), BF16),
            dma((8,)), dma((8,)),
            dma((2, 2)), dma((2, 2)),
            dma((8,)), dma((8,)),
            dma((2, 7)), dma((2, 8)),
            dma((2, 2, 2)), dma((2, 2, 2)),
            dma((2,)), dma((2,)),
            dma((2,)), dma((2,)),
            dma((2,)), dma((2,)),
        ],
        compiler_params=pltpu.CompilerParams(
            collective_id=0, has_side_effects=True, vmem_limit_bytes=60 * 2**20
        ),
    )(
        density.reshape(512, 192),
        w1.reshape(25, 120, 192),
        b1.reshape(1, 192),
        beta.reshape(1, 192),
        gamma,
        w2.reshape(27, 24, 192),
        b2.reshape(1, 192),
        w3.reshape(27, 24, 192),
        b3.reshape(1, 192),
    )
    return latent.reshape(1, 4, 16, 192), scales.reshape(1, 4, 16, 192)


def solution(mesh):
    in_specs = (
        P("wide", "narrow", None, None),
        P(None, None, None, "narrow", None),
        P(),
        P(),
        P(),
        P(None, None, None, "narrow", None),
        P(),
        P(None, None, None, "narrow", None),
        P(),
    )
    out_specs = (P("wide", "narrow", None, None), P("wide", "narrow", None, None))
    return jax.shard_map(
        on_device, mesh=mesh, in_specs=in_specs, out_specs=out_specs, check_vma=False
    )
```

```python
import jax
import jax.numpy as jnp
from jax import lax
from jax.experimental import pallas as pl
from jax.experimental.pallas import tpu as pltpu
from jax.sharding import PartitionSpec as P

MESH = pl.DeviceIdType.MESH
F32 = jnp.float32
BF16 = jnp.bfloat16

FAR = ((1, 2), (1, 1), (1, 3), (1, 0))
NEAR = ((0, 2), (0, 1), (0, 3))


def iota(shape, dim):
    return lax.broadcasted_iota(jnp.int32, shape, dim)


def rows_shifted(x, by):
    n = x.shape[0]
    col = iota(x.shape, 0) & 15
    if by == -1:
        return jnp.where(col == 0, 0.0, pltpu.roll(x, 1, 0))
    return jnp.where(col == 15, 0.0, pltpu.roll(x, n - 1, 0))


def kernel(
    x_in, w1_in, b1_in, beta_in, gamma_in, w2_in, b2_in, w3_in, b3_in,
    lat_ref, sc_ref,
    x_ref, w1_ref, b1_ref, beta_ref, gamma_ref, w2_ref, b2_ref, w3_ref, b3_ref, in_sem,
    send1, recv1, from_lo, from_hi, planes, w1k, acc, send2, recv2, wts,
    lat_p, lat_q, hid_p, hid_q,
    s1_send, s1_recv, f_send, f_recv, s2_send, s2_recv,
    g_send, g_recv, y_send, y_recv, c_send, c_recv, l_send, l_recv, h_send, h_recv,
):
    loads = [
        pltpu.make_async_copy(src, dst, in_sem.at[i])
        for i, (src, dst) in enumerate((
            (x_in, x_ref), (w2_in, w2_ref), (w3_in, w3_ref), (w1_in, w1_ref), (gamma_in, gamma_ref),
            (b1_in, b1_ref), (beta_in, beta_ref), (b2_in, b2_ref), (b3_in, b3_ref),
        ))
    ]
    for load in loads:
        load.start()
    w, n = lax.axis_index("wide"), lax.axis_index("narrow")
    wide = lax.axis_size("wide")
    zh, xx, core = n // 4, n % 4, w % 2
    yy = (w // 2) % 8
    y_up, y_down = w + 2 * ((yy + 1) % 8 - yy), w + 2 * ((yy + 7) % 8 - yy)
    quarter = 2 * core + yy % 2
    has_lo, has_hi = w > 0, w < wide - 1
    lo, hi = jnp.maximum(w - 1, 0), jnp.minimum(w + 1, wide - 1)
    sibling = w + 1 - 2 * core

    def peer(e, d):
        return ((zh + e) % 2) * 4 + (xx + d) % 4

    sent = []

    def send(src, dst, ssem, rsem, device, when=None):
        copy = pltpu.make_async_remote_copy(
            src_ref=src, dst_ref=dst, send_sem=ssem, recv_sem=rsem,
            device_id=device, device_id_type=MESH,
        )
        if when is None:
            copy.start()
        else:
            pl.when(when)(copy.start)
        sent.append((copy, when))

    def arrived(dst, rsem, when=None):
        copy = pltpu.make_async_remote_copy(
            src_ref=dst, dst_ref=dst, send_sem=rsem, recv_sem=rsem,
            device_id=(sibling, n), device_id_type=MESH,
        )
        if when is None:
            copy.wait_recv()
        else:
            pl.when(when)(copy.wait_recv)

    barrier = pltpu.get_barrier_semaphore()
    for e, d in FAR + NEAR:
        pl.semaphore_signal(barrier, inc=1, device_id=(w, peer(e, d)), device_id_type=MESH)

    for y in (y_up, y_down):
        pl.semaphore_signal(barrier, inc=1, device_id=(y, n), device_id_type=MESH)

    @pl.when(has_lo)
    def _():
        pl.semaphore_signal(barrier, inc=1, device_id=(lo, n), device_id_type=MESH)

    @pl.when(has_hi)
    def _():
        pl.semaphore_signal(barrier, inc=1, device_id=(hi, n), device_id_type=MESH)

    i, j = iota((256, 256), 0), iota((256, 256), 1)
    source = ((i >> 4) & 3) * 64 + (i >> 7) * 32 + (i & 15) * 2 + ((i >> 6) & 1)
    perm = jnp.where(j == source, 1.0, 0.0).astype(BF16)
    loads[0].wait()
    cut = [
        jnp.dot(perm, x_ref[256 * z : 256 * z + 256, :], preferred_element_type=F32)
        for z in range(2)
    ]
    parts = [
        jnp.concatenate([cut[z][64 * t : 64 * t + 64] for z in range(2)], axis=0) for t in range(4)
    ]
    blank = jnp.zeros((128, 64), F32)
    turned = [
        pltpu.roll(jnp.concatenate([parts[t], blank], axis=1), 24 * t, 1) if t else
        jnp.concatenate([parts[t], blank], axis=1)
        for t in range(4)
    ]
    lane = iota((128, 256), 1)
    for m in range(8):
        at = (lane - 24 * m) & 255
        block = jnp.where(at < 24, turned[0], jnp.where(at < 48, turned[1], jnp.where(at < 72, turned[2], turned[3])))
        block = pltpu.roll(block, (256 - 24 * m) % 256, 1)[:, :128] if m else block[:, :128]
        block = jnp.where(lane[:, :128] < 96, block, 0.0)
        first, second = block[:64], pltpu.roll(block[64:], 96, 1)
        ln = iota((64, 128), 1)
        rest = jnp.where(ln[:32] < 64, second[:32], pltpu.roll(second[32:], 64, 1))
        send1[m] = jnp.concatenate([jnp.where(ln < 96, first, second), rest], axis=0).astype(BF16)

    pl.semaphore_wait(barrier, 9 + has_lo.astype(jnp.int32) + has_hi.astype(jnp.int32))

    for e, d in FAR + NEAR:
        m = peer(e, d)
        send(send1.at[m], recv1.at[n], s1_send.at[m], s1_recv.at[n], (w, m))
    recv1[n] = send1[n]

    for load in loads[1:]:
        load.wait()

    for layer, ref in ((0, w2_ref), (1, w3_ref)):

        @pl.loop(0, 11)
        def _(t, layer=layer, ref=ref):
            at = 11 * quarter + t
            tap, kind = 2 * (at // 3), at % 3
            even = ref[jnp.minimum(tap, 26)].astype(F32)
            odd = ref[jnp.minimum(tap + 1, 26)].astype(F32)
            odd = jnp.where(tap + 1 < 27, odd, 0.0)
            both = jnp.concatenate([even[:, 128:], odd[:, 128:]], axis=1)
            value = jnp.where(kind == 0, even[:, :128], jnp.where(kind == 1, odd[:, :128], both))
            wts[layer, at, n] = value.astype(BF16)

    mirror = peer(1, 0)

    def slice_of(layer, m):
        return wts.at[layer, pl.ds(11 * quarter, 11), m]

    def to_peers(layer):
        part = slice_of(layer, n)
        for at, (e, d) in enumerate(((1, 0),) + NEAR):
            send(part, part, g_send.at[layer, at], g_recv.at[layer, n], (w, peer(e, d)))

    def forward(layer):
        part = slice_of(layer, mirror)
        arrived(part, g_recv.at[layer, mirror])
        for at, (e, d) in enumerate(NEAR):
            send(part, part, g_send.at[layer, 4 + at], g_recv.at[layer, mirror], (w, peer(e, d)))

    def y_part(layer, q, up, half):
        return wts.at[layer, pl.ds(11 * q + (0 if up else 6), 6 if up else 5), pl.ds(4 * half, 4)]

    def along_y(layer, turn):
        for e, d in NEAR if turn == 0 else FAR[:3]:
            m = peer(e, d)
            arrived(slice_of(layer, m), g_recv.at[layer, m])
        half = (zh + turn) % 2
        for up, y in ((1, y_up), (0, y_down)):
            part = y_part(layer, quarter, up, half)
            send(part, part, y_send.at[layer, turn, up], y_recv.at[layer, turn, up], (y, n))

    def to_sibling(layer):
        for turn in range(2):
            for up in (1, 0):
                part = y_part(layer, quarter + 1 - 2 * (yy % 2), up, (zh + turn) % 2)
                arrived(part, y_recv.at[layer, turn, up])
        part = wts.at[layer, pl.ds(22 * core, 22)]
        send(part, part, c_send.at[layer], c_recv.at[layer], (sibling, n))

    to_peers(0)
    to_peers(1)

    w1k[...] = jnp.zeros_like(w1k)

    def fill(a, odd):
        for b in range(5):
            step, rp = b // 2, b % 2
            at = a * 3 + step
            v = w1_ref[a * 5 + b].astype(F32)
            last = jnp.concatenate([v[96:120], jnp.zeros((8, 192), F32)], axis=0)
            for base, rows in ((0, v[0:48]), (128, v[48:96])):
                rows = rows.astype(BF16)
                if not odd:
                    w1k[at, base + 48 * rp : base + 48 * rp + 48, 0:192] = rows
                elif rp == 0:
                    w1k[at, base + 96 : base + 128, 0:192] = rows[0:32]
                    w1k[at, base : base + 16, 0:192] = rows[32:48]
                else:
                    w1k[at, base + 16 : base + 64, 0:192] = rows
            gap = 128 * rp + (64 if odd else 96)
            w1k[at, gap : gap + 32, 0:192] = last.astype(BF16)

    @pl.loop(0, 3)
    def _(t):
        fill(2 * t, False)

    @pl.loop(0, 2)
    def _(t):
        fill(2 * t + 1, True)

    planes[:, 0:16, :] = jnp.zeros((5, 16, 256), BF16)
    planes[:, 528:544, :] = jnp.zeros((5, 16, 256), BF16)
    acc[0:32, :] = jnp.zeros((32, 256), F32)
    acc[544:576, :] = jnp.zeros((32, 256), F32)

    for turn in range(2):
        for e, d in NEAR if turn == 0 else FAR:
            m = peer(e, d)
            arrived(recv1.at[m], s1_recv.at[m])
        g = (zh + turn) % 2
        four = pl.ds(4 * g, 4)
        send(recv1.at[four], from_lo.at[four], f_send.at[0, turn], f_recv.at[0, g], (hi, n), has_hi)
        send(
            recv1.at[four, 0:64], from_hi.at[four], f_send.at[1, turn], f_recv.at[1, g], (lo, n), has_lo
        )

    def build(a, read, begin=0, count=8):
        @pl.loop(0, count, unroll=count // 2)
        def _(step):
            blk = begin + step
            x = read(blk).astype(F32)
            ln = iota((64, 128), 1)
            kept = ln < 96
            if a % 2:
                rest = jnp.concatenate([x[64:], pltpu.roll(x[64:], 64, 1)], axis=0)
                x = jnp.where(kept, rest, x[:64])
                kept = (ln < 64) | (ln >= 96)
            after = rows_shifted(x, 1)
            before = jnp.where(kept, rows_shifted(x, -1), pltpu.roll(after, 96, 1))
            same = jnp.where(kept, x, pltpu.roll(after, 48, 1))
            at = pl.ds(pl.multiple_of(16 + 64 * blk, 16), 64)
            planes[a, at, 0:128] = before.astype(BF16)
            planes[a, at, 128:256] = same.astype(BF16)

    def product(a, first=0, size=512):
        rows = jnp.concatenate(
            [planes[a, pl.ds(first + 16 * s, size), :] for s in range(3)], axis=1
        )
        return jnp.dot(
            rows, w1k[3 * a : 3 * a + 3].reshape(768, 256), preferred_element_type=F32
        )

    along_y(0, 0)
    build(2, lambda blk: recv1[blk, 0:64])
    build(3, lambda blk: recv1[blk])
    acc[32:544, :] = product(2) + product(3)

    @pl.when(jnp.logical_not(has_lo))
    def _():
        from_lo[...] = jnp.zeros_like(from_lo)

    @pl.when(jnp.logical_not(has_hi))
    def _():
        from_hi[...] = jnp.zeros_like(from_hi)

    for turn in range(2):
        g = (zh + turn) % 2
        four = pl.ds(4 * g, 4)
        arrived(from_lo.at[four], f_recv.at[0, g], has_lo)
        arrived(from_hi.at[four], f_recv.at[1, g], has_hi)
        if turn == 0:
            forward(0)
        else:
            forward(1)
            along_y(1, 0)
        build(0, lambda blk: from_lo[blk, 0:64], 4 * g, 4)
        build(1, lambda blk: from_lo[blk], 4 * g, 4)
        build(4, lambda blk: from_hi[blk], 4 * g, 4)
        size = (240, 272)[turn]
        first = pl.multiple_of(zh * 272 if turn == 0 else (1 - zh) * 240, 16)
        add = product(0, first, size) + product(1, first, size) + product(4, first, size)
        acc[pl.ds(pl.multiple_of(32 + first, 16), size), :] += add

    def packed(at):
        rows = acc[at, :]
        left, right = rows[:, :128], rows[:, 128:]
        ln = iota((64, 128), 1)
        side = jnp.where(ln < 64, right[:64], pltpu.roll(right[64:], 64, 1))
        return jnp.concatenate([left, side], axis=0)

    @pl.loop(0, 8)
    def _(m):
        send2[m] = packed(pl.ds(pl.multiple_of(64 * m, 64), 128)).astype(BF16)

    for e, d in FAR + NEAR:
        m = peer(e, d)
        send(send2.at[m], recv2.at[n], s2_send.at[m], s2_recv.at[n], (w, m))
    along_y(0, 1)
    along_y(1, 1)
    to_sibling(0)

    total = packed(pl.ds(pl.multiple_of(64 * n, 64), 128))
    for e, d in NEAR + FAR:
        m = peer(e, d)
        arrived(recv2.at[m], s2_recv.at[m])
        total = total + recv2[m].astype(F32)
    side = total[128:192]
    side = jnp.concatenate([side, pltpu.roll(side, 64, 1)], axis=0)
    conv = jnp.concatenate([total[:128], side[:, :64]], axis=1) + b1_ref[...]
    denom = beta_ref[...] + jnp.dot(
        conv * conv, gamma_ref[...], precision=lax.Precision.HIGHEST, preferred_element_type=F32
    )
    latent = (conv * lax.rsqrt(denom)).astype(BF16)
    lat_ref[...] = latent[32:96]

    def inside(values, first):
        row = first + (iota(values.shape, 0) >> 4)
        return jnp.where((row >= 0) & (row < 32), values, 0.0).astype(BF16)

    def exchange(buf, ssem, rsem):
        send(buf.at[1], buf.at[0], ssem.at[0], rsem.at[0], (hi, n), has_hi)
        send(buf.at[1], buf.at[2], ssem.at[1], rsem.at[1], (lo, n), has_lo)

    def kernel_of(layer, at):
        return wts[layer, at].reshape(192, 128)

    def layer_of(layer, buf, buf_q, rsem, rows):
        def shifts(z):
            x = buf[z].astype(F32)
            buf_q[z, 0] = rows_shifted(x, -1).astype(BF16)
            buf_q[z, 1] = rows_shifted(x, 1).astype(BF16)

        sums = [jnp.zeros((rows, 256), F32)] * 2

        def taps(z, first):
            for j in range(9):
                b, c = j // 3, j % 3
                at = pl.ds(16 * b, rows)
                left = buf[z, at, :] if c == 1 else buf_q[z, c // 2, at, :]
                if z is one:
                    pair, odd = (9 + j) // 2, (9 + j) % 2
                else:
                    pair, odd = first + j // 2, j % 2
                kern = jnp.concatenate(
                    [kernel_of(layer, 3 * pair + odd), kernel_of(layer, 3 * pair + 2)], axis=1
                )
                sums[odd] += jnp.dot(left, kern, preferred_element_type=F32)

        one = 1
        shifts(one)
        taps(one, None)
        near = 2 * (1 - core)
        far = 2 - near
        has_far = jnp.where(core == 0, has_lo.astype(jnp.int32), has_hi.astype(jnp.int32)) == 1

        @pl.when(jnp.logical_not(has_far))
        def _():
            buf[far] = jnp.zeros((buf.shape[1], 192), BF16)

        arrived(buf.at[near], rsem.at[1 - core])
        shifts(near)
        taps(near, 9 * (1 - core))
        arrived(buf.at[far], rsem.at[core], has_far)
        shifts(far)
        taps(far, 9 * core)
        even, odd = sums
        side = even[:, 128:] + pltpu.roll(odd[:, 128:], 64, 1)
        return jnp.concatenate([even[:, :128] + odd[:, :128], side[:, :64]], axis=1)

    lat_p[1] = inside(jnp.abs(latent.astype(F32)), 4 * n - 2)
    exchange(lat_p, l_send, l_recv)
    other = pl.ds(22 * (1 - core), 22)
    arrived(wts.at[0, other], c_recv.at[0])
    to_sibling(1)
    hidden = jnp.maximum(layer_of(0, lat_p, lat_q, l_recv, 96) + b2_ref[...], 0.0)
    hid_p[1] = inside(hidden, 4 * n - 1)
    exchange(hid_p, h_send, h_recv)
    arrived(wts.at[1, other], c_recv.at[1])
    s = layer_of(1, hid_p, hid_q, h_recv, 64) + b3_ref[...]
    sc_ref[...] = 0.11 + (jnp.maximum(s, 0.0) + jnp.log1p(jnp.exp(-jnp.abs(s))))

    for copy, when in sent:
        if when is None:
            copy.wait_send()
        else:
            pl.when(when)(copy.wait_send)


def on_device(density, w1, b1, beta, gamma, w2, b2, w3, b3):
    vmem = pl.BlockSpec(memory_space=pltpu.VMEM)
    dma = pltpu.SemaphoreType.DMA
    latent, scales = pl.pallas_call(
        kernel,
        out_shape=(
            jax.ShapeDtypeStruct((64, 192), BF16),
            jax.ShapeDtypeStruct((64, 192), F32),
        ),
        in_specs=[pl.BlockSpec(memory_space=pl.ANY)] * 9,
        out_specs=(vmem, vmem),
        scratch_shapes=[
            pltpu.VMEM((512, 192), BF16),
            pltpu.VMEM((25, 120, 192), BF16),
            pltpu.VMEM((1, 192), F32),
            pltpu.VMEM((1, 192), F32),
            pltpu.VMEM((192, 192), F32),
            pltpu.VMEM((27, 24, 192), BF16),
            pltpu.VMEM((1, 192), F32),
            pltpu.VMEM((27, 24, 192), BF16),
            pltpu.VMEM((1, 192), F32),
            dma((9,)),
            pltpu.VMEM((8, 96, 128), BF16),
            pltpu.VMEM((8, 96, 128), BF16),
            pltpu.VMEM((8, 96, 128), BF16),
            pltpu.VMEM((8, 64, 128), BF16),
            pltpu.VMEM((5, 544, 256), BF16),
            pltpu.VMEM((15, 256, 256), BF16),
            pltpu.VMEM((576, 256), F32),
            pltpu.VMEM((8, 192, 128), BF16),
            pltpu.VMEM((8, 192, 128), BF16),
            pltpu.VMEM((2, 44, 8, 24, 128), BF16),
            pltpu.VMEM((3, 128, 192), BF16),
            pltpu.VMEM((3, 2, 128, 192), BF16),
            pltpu.VMEM((3, 96, 192), BF16),
            pltpu.VMEM((3, 2, 96, 192), BF16),
            dma((8,)), dma((8,)),
            dma((2, 2)), dma((2, 2)),
            dma((8,)), dma((8,)),
            dma((2, 7)), dma((2, 8)),
            dma((2, 2, 2)), dma((2, 2, 2)),
            dma((2,)), dma((2,)),
            dma((2,)), dma((2,)),
            dma((2,)), dma((2,)),
        ],
        compiler_params=pltpu.CompilerParams(
            collective_id=0, has_side_effects=True, vmem_limit_bytes=60 * 2**20
        ),
    )(
        density.reshape(512, 192),
        w1.reshape(25, 120, 192),
        b1.reshape(1, 192),
        beta.reshape(1, 192),
        gamma,
        w2.reshape(27, 24, 192),
        b2.reshape(1, 192),
        w3.reshape(27, 24, 192),
        b3.reshape(1, 192),
    )
    return latent.reshape(1, 4, 16, 192), scales.reshape(1, 4, 16, 192)


def solution(mesh):
    in_specs = (
        P("wide", "narrow", None, None),
        P(None, None, None, "narrow", None),
        P(),
        P(),
        P(),
        P(None, None, None, "narrow", None),
        P(),
        P(None, None, None, "narrow", None),
        P(),
    )
    out_specs = (P("wide", "narrow", None, None), P("wide", "narrow", None, None))
    return jax.shard_map(
        on_device, mesh=mesh, in_specs=in_specs, out_specs=out_specs, check_vma=False
    )
```

```python
import jax
import jax.numpy as jnp
from jax import lax
from jax.experimental import pallas as pl
from jax.experimental.pallas import tpu as pltpu
from jax.sharding import PartitionSpec as P

MESH = pl.DeviceIdType.MESH
F32 = jnp.float32
BF16 = jnp.bfloat16

FAR = ((1, 2), (1, 1), (1, 3), (1, 0))
NEAR = ((0, 2), (0, 1), (0, 3))


def iota(shape, dim):
    return lax.broadcasted_iota(jnp.int32, shape, dim)


def rows_shifted(x, by):
    n = x.shape[0]
    col = iota(x.shape, 0) & 15
    if by == -1:
        return jnp.where(col == 0, 0.0, pltpu.roll(x, 1, 0))
    return jnp.where(col == 15, 0.0, pltpu.roll(x, n - 1, 0))


def kernel(
    x_in, w1_in, b1_in, beta_in, gamma_in, w2_in, b2_in, w3_in, b3_in,
    lat_ref, sc_ref,
    x_ref, w1_ref, b1_ref, beta_ref, gamma_ref, w2_ref, b2_ref, w3_ref, b3_ref, in_sem,
    send1, recv1, from_lo, from_hi, planes, w1k, acc, send2, recv2, wts,
    lat_p, lat_q, hid_p, hid_q,
    s1_send, s1_recv, f_send, f_recv, s2_send, s2_recv,
    g_send, g_recv, y_send, y_recv, c_send, c_recv, l_send, l_recv, h_send, h_recv,
):
    loads = [
        pltpu.make_async_copy(src, dst, in_sem.at[i])
        for i, (src, dst) in enumerate((
            (x_in, x_ref), (w2_in, w2_ref), (w3_in, w3_ref), (w1_in, w1_ref), (gamma_in, gamma_ref),
            (b1_in, b1_ref), (beta_in, beta_ref), (b2_in, b2_ref), (b3_in, b3_ref),
        ))
    ]
    loads[0].start()
    w, n = lax.axis_index("wide"), lax.axis_index("narrow")
    wide = lax.axis_size("wide")
    zh, xx, core = n // 4, n % 4, w % 2
    yy = (w // 2) % 8
    y_up, y_down = w + 2 * ((yy + 1) % 8 - yy), w + 2 * ((yy + 7) % 8 - yy)
    quarter = 2 * core + yy % 2
    has_lo, has_hi = w > 0, w < wide - 1
    lo, hi = jnp.maximum(w - 1, 0), jnp.minimum(w + 1, wide - 1)
    sibling = w + 1 - 2 * core

    def peer(e, d):
        return ((zh + e) % 2) * 4 + (xx + d) % 4

    sent = []

    def send(src, dst, ssem, rsem, device, when=None):
        copy = pltpu.make_async_remote_copy(
            src_ref=src, dst_ref=dst, send_sem=ssem, recv_sem=rsem,
            device_id=device, device_id_type=MESH,
        )
        if when is None:
            copy.start()
        else:
            pl.when(when)(copy.start)
        sent.append((copy, when))

    def arrived(dst, rsem, when=None):
        copy = pltpu.make_async_remote_copy(
            src_ref=dst, dst_ref=dst, send_sem=rsem, recv_sem=rsem,
            device_id=(sibling, n), device_id_type=MESH,
        )
        if when is None:
            copy.wait_recv()
        else:
            pl.when(when)(copy.wait_recv)

    barrier = pltpu.get_barrier_semaphore()
    for e, d in FAR + NEAR:
        pl.semaphore_signal(barrier, inc=1, device_id=(w, peer(e, d)), device_id_type=MESH)

    for y in (y_up, y_down):
        pl.semaphore_signal(barrier, inc=1, device_id=(y, n), device_id_type=MESH)

    @pl.when(has_lo)
    def _():
        pl.semaphore_signal(barrier, inc=1, device_id=(lo, n), device_id_type=MESH)

    @pl.when(has_hi)
    def _():
        pl.semaphore_signal(barrier, inc=1, device_id=(hi, n), device_id_type=MESH)

    i, j = iota((256, 256), 0), iota((256, 256), 1)
    source = ((i >> 4) & 3) * 64 + (i >> 7) * 32 + (i & 15) * 2 + ((i >> 6) & 1)
    perm = jnp.where(j == source, 1.0, 0.0).astype(BF16)
    loads[0].wait()
    for load in loads[1:]:
        load.start()
    cut = [
        jnp.dot(perm, x_ref[256 * z : 256 * z + 256, :], preferred_element_type=F32)
        for z in range(2)
    ]
    parts = [
        jnp.concatenate([cut[z][64 * t : 64 * t + 64] for z in range(2)], axis=0) for t in range(4)
    ]
    blank = jnp.zeros((128, 64), F32)
    turned = [
        pltpu.roll(jnp.concatenate([parts[t], blank], axis=1), 24 * t, 1) if t else
        jnp.concatenate([parts[t], blank], axis=1)
        for t in range(4)
    ]
    lane = iota((128, 256), 1)
    for m in range(8):
        at = (lane - 24 * m) & 255
        block = jnp.where(at < 24, turned[0], jnp.where(at < 48, turned[1], jnp.where(at < 72, turned[2], turned[3])))
        block = pltpu.roll(block, (256 - 24 * m) % 256, 1)[:, :128] if m else block[:, :128]
        block = jnp.where(lane[:, :128] < 96, block, 0.0)
        first, second = block[:64], pltpu.roll(block[64:], 96, 1)
        ln = iota((64, 128), 1)
        rest = jnp.where(ln[:32] < 64, second[:32], pltpu.roll(second[32:], 64, 1))
        send1[m] = jnp.concatenate([jnp.where(ln < 96, first, second), rest], axis=0).astype(BF16)

    pl.semaphore_wait(barrier, 9 + has_lo.astype(jnp.int32) + has_hi.astype(jnp.int32))

    for e, d in FAR + NEAR:
        m = peer(e, d)
        send(send1.at[m], recv1.at[n], s1_send.at[m], s1_recv.at[n], (w, m))
    recv1[n] = send1[n]

    for load in loads[1:]:
        load.wait()

    for layer, ref in ((0, w2_ref), (1, w3_ref)):

        @pl.loop(0, 11)
        def _(t, layer=layer, ref=ref):
            at = 11 * quarter + t
            tap, kind = 2 * (at // 3), at % 3
            even = ref[jnp.minimum(tap, 26)].astype(F32)
            odd = ref[jnp.minimum(tap + 1, 26)].astype(F32)
            odd = jnp.where(tap + 1 < 27, odd, 0.0)
            both = jnp.concatenate([even[:, 128:], odd[:, 128:]], axis=1)
            value = jnp.where(kind == 0, even[:, :128], jnp.where(kind == 1, odd[:, :128], both))
            wts[layer, at, n] = value.astype(BF16)

    mirror = peer(1, 0)

    def slice_of(layer, m):
        return wts.at[layer, pl.ds(11 * quarter, 11), m]

    def to_peers(layer):
        part = slice_of(layer, n)
        for at, (e, d) in enumerate(((1, 0),) + NEAR):
            send(part, part, g_send.at[layer, at], g_recv.at[layer, n], (w, peer(e, d)))

    def forward(layer):
        part = slice_of(layer, mirror)
        arrived(part, g_recv.at[layer, mirror])
        for at, (e, d) in enumerate(NEAR):
            send(part, part, g_send.at[layer, 4 + at], g_recv.at[layer, mirror], (w, peer(e, d)))

    def y_part(layer, q, up, half):
        return wts.at[layer, pl.ds(11 * q + (0 if up else 6), 6 if up else 5), pl.ds(4 * half, 4)]

    def along_y(layer, turn):
        for e, d in NEAR if turn == 0 else FAR[:3]:
            m = peer(e, d)
            arrived(slice_of(layer, m), g_recv.at[layer, m])
        half = (zh + turn) % 2
        for up, y in ((1, y_up), (0, y_down)):
            part = y_part(layer, quarter, up, half)
            send(part, part, y_send.at[layer, turn, up], y_recv.at[layer, turn, up], (y, n))

    def to_sibling(layer):
        for turn in range(2):
            for up in (1, 0):
                part = y_part(layer, quarter + 1 - 2 * (yy % 2), up, (zh + turn) % 2)
                arrived(part, y_recv.at[layer, turn, up])
        part = wts.at[layer, pl.ds(22 * core, 22)]
        send(part, part, c_send.at[layer], c_recv.at[layer], (sibling, n))

    to_peers(0)
    to_peers(1)

    w1k[...] = jnp.zeros_like(w1k)

    def fill(a, odd):
        for b in range(5):
            step, rp = b // 2, b % 2
            at = a * 3 + step
            v = w1_ref[a * 5 + b].astype(F32)
            last = jnp.concatenate([v[96:120], jnp.zeros((8, 192), F32)], axis=0)
            for base, rows in ((0, v[0:48]), (128, v[48:96])):
                rows = rows.astype(BF16)
                if not odd:
                    w1k[at, base + 48 * rp : base + 48 * rp + 48, 0:192] = rows
                elif rp == 0:
                    w1k[at, base + 96 : base + 128, 0:192] = rows[0:32]
                    w1k[at, base : base + 16, 0:192] = rows[32:48]
                else:
                    w1k[at, base + 16 : base + 64, 0:192] = rows
            gap = 128 * rp + (64 if odd else 96)
            w1k[at, gap : gap + 32, 0:192] = last.astype(BF16)

    @pl.loop(0, 3)
    def _(t):
        fill(2 * t, False)

    @pl.loop(0, 2)
    def _(t):
        fill(2 * t + 1, True)

    planes[:, 0:16, :] = jnp.zeros((5, 16, 256), BF16)
    planes[:, 528:544, :] = jnp.zeros((5, 16, 256), BF16)
    acc[0:32, :] = jnp.zeros((32, 256), F32)
    acc[544:576, :] = jnp.zeros((32, 256), F32)

    for turn in range(2):
        for e, d in NEAR if turn == 0 else FAR:
            m = peer(e, d)
            arrived(recv1.at[m], s1_recv.at[m])
        g = (zh + turn) % 2
        four = pl.ds(4 * g, 4)
        send(recv1.at[four], from_lo.at[four], f_send.at[0, turn], f_recv.at[0, g], (hi, n), has_hi)
        send(
            recv1.at[four, 0:64], from_hi.at[four], f_send.at[1, turn], f_recv.at[1, g], (lo, n), has_lo
        )

    def build(a, read, begin=0, count=8):
        @pl.loop(0, count, unroll=count // 2)
        def _(step):
            blk = begin + step
            x = read(blk).astype(F32)
            ln = iota((64, 128), 1)
            kept = ln < 96
            if a % 2:
                rest = jnp.concatenate([x[64:], pltpu.roll(x[64:], 64, 1)], axis=0)
                x = jnp.where(kept, rest, x[:64])
                kept = (ln < 64) | (ln >= 96)
            after = rows_shifted(x, 1)
            before = jnp.where(kept, rows_shifted(x, -1), pltpu.roll(after, 96, 1))
            same = jnp.where(kept, x, pltpu.roll(after, 48, 1))
            at = pl.ds(pl.multiple_of(16 + 64 * blk, 16), 64)
            planes[a, at, 0:128] = before.astype(BF16)
            planes[a, at, 128:256] = same.astype(BF16)

    def product(a, first=0, size=512):
        rows = jnp.concatenate(
            [planes[a, pl.ds(first + 16 * s, size), :] for s in range(3)], axis=1
        )
        return jnp.dot(
            rows, w1k[3 * a : 3 * a + 3].reshape(768, 256), preferred_element_type=F32
        )

    along_y(0, 0)
    build(2, lambda blk: recv1[blk, 0:64])
    build(3, lambda blk: recv1[blk])
    acc[32:544, :] = product(2) + product(3)

    @pl.when(jnp.logical_not(has_lo))
    def _():
        from_lo[...] = jnp.zeros_like(from_lo)

    @pl.when(jnp.logical_not(has_hi))
    def _():
        from_hi[...] = jnp.zeros_like(from_hi)

    for turn in range(2):
        g = (zh + turn) % 2
        four = pl.ds(4 * g, 4)
        arrived(from_lo.at[four], f_recv.at[0, g], has_lo)
        arrived(from_hi.at[four], f_recv.at[1, g], has_hi)
        if turn == 0:
            forward(0)
        build(0, lambda blk: from_lo[blk, 0:64], 4 * g, 4)
        build(1, lambda blk: from_lo[blk], 4 * g, 4)
        build(4, lambda blk: from_hi[blk], 4 * g, 4)
        size = (240, 272)[turn]
        first = pl.multiple_of(zh * 272 if turn == 0 else (1 - zh) * 240, 16)
        add = product(0, first, size) + product(1, first, size) + product(4, first, size)
        acc[pl.ds(pl.multiple_of(32 + first, 16), size), :] += add

    def packed(at):
        rows = acc[at, :]
        left, right = rows[:, :128], rows[:, 128:]
        ln = iota((64, 128), 1)
        side = jnp.where(ln < 64, right[:64], pltpu.roll(right[64:], 64, 1))
        return jnp.concatenate([left, side], axis=0)

    for e, d in FAR + NEAR:
        m = peer(e, d)
        send2[m] = packed(pl.ds(pl.multiple_of(64 * m, 64), 128)).astype(BF16)
        send(send2.at[m], recv2.at[n], s2_send.at[m], s2_recv.at[n], (w, m))
    forward(1)
    along_y(1, 0)
    along_y(0, 1)
    along_y(1, 1)
    to_sibling(0)

    total = packed(pl.ds(pl.multiple_of(64 * n, 64), 128))
    for e, d in NEAR + FAR:
        m = peer(e, d)
        arrived(recv2.at[m], s2_recv.at[m])
        total = total + recv2[m].astype(F32)
    side = total[128:192]
    side = jnp.concatenate([side, pltpu.roll(side, 64, 1)], axis=0)
    conv = jnp.concatenate([total[:128], side[:, :64]], axis=1) + b1_ref[...]
    denom = beta_ref[...] + jnp.dot(
        conv * conv, gamma_ref[...], precision=lax.Precision.HIGHEST, preferred_element_type=F32
    )
    latent = (conv * lax.rsqrt(denom)).astype(BF16)

    def inside(values, first):
        row = first + (iota(values.shape, 0) >> 4)
        return jnp.where((row >= 0) & (row < 32), values, 0.0).astype(BF16)

    def exchange(buf, ssem, rsem):
        send(buf.at[1], buf.at[0], ssem.at[0], rsem.at[0], (hi, n), has_hi)
        send(buf.at[1], buf.at[2], ssem.at[1], rsem.at[1], (lo, n), has_lo)

    def kernel_of(layer, at):
        return wts[layer, at].reshape(192, 128)

    def layer_of(layer, buf, buf_q, rsem, rows):
        def shifts(z):
            x = buf[z].astype(F32)
            buf_q[z, 0] = rows_shifted(x, -1).astype(BF16)
            buf_q[z, 1] = rows_shifted(x, 1).astype(BF16)

        sums = [jnp.zeros((rows, 256), F32)] * 2

        def taps(z, first):
            for j in range(9):
                b, c = j // 3, j % 3
                at = pl.ds(16 * b, rows)
                left = buf[z, at, :] if c == 1 else buf_q[z, c // 2, at, :]
                if z is one:
                    pair, odd = (9 + j) // 2, (9 + j) % 2
                else:
                    pair, odd = first + j // 2, j % 2
                kern = jnp.concatenate(
                    [kernel_of(layer, 3 * pair + odd), kernel_of(layer, 3 * pair + 2)], axis=1
                )
                sums[odd] += jnp.dot(left, kern, preferred_element_type=F32)

        one = 1
        shifts(one)
        taps(one, None)
        near = 2 * (1 - core)
        far = 2 - near
        has_far = jnp.where(core == 0, has_lo.astype(jnp.int32), has_hi.astype(jnp.int32)) == 1

        @pl.when(jnp.logical_not(has_far))
        def _():
            buf[far] = jnp.zeros((buf.shape[1], 192), BF16)

        arrived(buf.at[near], rsem.at[1 - core])
        shifts(near)
        taps(near, 9 * (1 - core))
        if layer == 0:
            to_sibling(1)
        arrived(buf.at[far], rsem.at[core], has_far)
        shifts(far)
        taps(far, 9 * core)
        even, odd = sums
        side = even[:, 128:] + pltpu.roll(odd[:, 128:], 64, 1)
        return jnp.concatenate([even[:, :128] + odd[:, :128], side[:, :64]], axis=1)

    lat_p[1] = inside(jnp.abs(latent.astype(F32)), 4 * n - 2)
    exchange(lat_p, l_send, l_recv)
    lat_ref[...] = latent[32:96]
    other = pl.ds(22 * (1 - core), 22)
    arrived(wts.at[0, other], c_recv.at[0])
    hidden = jnp.maximum(layer_of(0, lat_p, lat_q, l_recv, 96) + b2_ref[...], 0.0)
    hid_p[1] = inside(hidden, 4 * n - 1)
    exchange(hid_p, h_send, h_recv)
    arrived(wts.at[1, other], c_recv.at[1])
    s = layer_of(1, hid_p, hid_q, h_recv, 64) + b3_ref[...]
    sc_ref[...] = s

    for copy, when in sent:
        if when is None:
            copy.wait_send()
        else:
            pl.when(when)(copy.wait_send)


def finish(lat_in, s_in, lat_ref, sc_ref):
    lat_ref[...] = lat_in[...]
    s = s_in[...]
    sc_ref[...] = 0.11 + (jnp.maximum(s, 0.0) + jnp.log1p(jnp.exp(-jnp.abs(s))))


def on_device(density, w1, b1, beta, gamma, w2, b2, w3, b3):
    vmem = pl.BlockSpec(memory_space=pltpu.VMEM)
    dma = pltpu.SemaphoreType.DMA
    latent, scales = pl.pallas_call(
        kernel,
        out_shape=(
            jax.ShapeDtypeStruct((64, 192), BF16),
            jax.ShapeDtypeStruct((64, 192), F32),
        ),
        in_specs=[pl.BlockSpec(memory_space=pl.ANY)] * 9,
        out_specs=(vmem, vmem),
        scratch_shapes=[
            pltpu.VMEM((512, 192), BF16),
            pltpu.VMEM((25, 120, 192), BF16),
            pltpu.VMEM((1, 192), F32),
            pltpu.VMEM((1, 192), F32),
            pltpu.VMEM((192, 192), F32),
            pltpu.VMEM((27, 24, 192), BF16),
            pltpu.VMEM((1, 192), F32),
            pltpu.VMEM((27, 24, 192), BF16),
            pltpu.VMEM((1, 192), F32),
            dma((9,)),
            pltpu.VMEM((8, 96, 128), BF16),
            pltpu.VMEM((8, 96, 128), BF16),
            pltpu.VMEM((8, 96, 128), BF16),
            pltpu.VMEM((8, 64, 128), BF16),
            pltpu.VMEM((5, 544, 256), BF16),
            pltpu.VMEM((15, 256, 256), BF16),
            pltpu.VMEM((576, 256), F32),
            pltpu.VMEM((8, 192, 128), BF16),
            pltpu.VMEM((8, 192, 128), BF16),
            pltpu.VMEM((2, 44, 8, 24, 128), BF16),
            pltpu.VMEM((3, 128, 192), BF16),
            pltpu.VMEM((3, 2, 128, 192), BF16),
            pltpu.VMEM((3, 96, 192), BF16),
            pltpu.VMEM((3, 2, 96, 192), BF16),
            dma((8,)), dma((8,)),
            dma((2, 2)), dma((2, 2)),
            dma((8,)), dma((8,)),
            dma((2, 7)), dma((2, 8)),
            dma((2, 2, 2)), dma((2, 2, 2)),
            dma((2,)), dma((2,)),
            dma((2,)), dma((2,)),
            dma((2,)), dma((2,)),
        ],
        compiler_params=pltpu.CompilerParams(
            collective_id=0, has_side_effects=True, vmem_limit_bytes=60 * 2**20
        ),
    )(
        density.reshape(512, 192),
        w1.reshape(25, 120, 192),
        b1.reshape(1, 192),
        beta.reshape(1, 192),
        gamma,
        w2.reshape(27, 24, 192),
        b2.reshape(1, 192),
        w3.reshape(27, 24, 192),
        b3.reshape(1, 192),
    )
    latent, scales = pl.pallas_call(
        finish,
        out_shape=(
            jax.ShapeDtypeStruct((64, 192), BF16),
            jax.ShapeDtypeStruct((64, 192), F32),
        ),
        in_specs=[vmem] * 2,
        out_specs=(vmem, vmem),
    )(latent, scales)
    return latent.reshape(1, 4, 16, 192), scales.reshape(1, 4, 16, 192)


def solution(mesh):
    in_specs = (
        P("wide", "narrow", None, None),
        P(None, None, None, "narrow", None),
        P(),
        P(),
        P(),
        P(None, None, None, "narrow", None),
        P(),
        P(None, None, None, "narrow", None),
        P(),
    )
    out_specs = (P("wide", "narrow", None, None), P("wide", "narrow", None, None))
    return jax.shard_map(
        on_device, mesh=mesh, in_specs=in_specs, out_specs=out_specs, check_vma=False
    )
```

```python
import jax
import jax.numpy as jnp
from jax import lax
from jax.experimental import pallas as pl
from jax.experimental.pallas import tpu as pltpu
from jax.sharding import PartitionSpec as P

MESH = pl.DeviceIdType.MESH
F32 = jnp.float32
BF16 = jnp.bfloat16

FAR = ((1, 2), (1, 1), (1, 3), (1, 0))
NEAR = ((0, 2), (0, 1), (0, 3))


def iota(shape, dim):
    return lax.broadcasted_iota(jnp.int32, shape, dim)


def rows_shifted(x, by):
    n = x.shape[0]
    col = iota(x.shape, 0) & 15
    if by == -1:
        return jnp.where(col == 0, 0.0, pltpu.roll(x, 1, 0))
    return jnp.where(col == 15, 0.0, pltpu.roll(x, n - 1, 0))


def kernel(
    x_in, w1_in, b1_in, beta_in, gamma_in, w2_in, b2_in, w3_in, b3_in,
    lat_ref, sc_ref,
    x_ref, w1_ref, b1_ref, beta_ref, gamma_ref, w2_ref, b2_ref, w3_ref, b3_ref, in_sem,
    send1, recv1, from_lo, from_hi, planes, w1k, acc, send2, recv2, wts,
    lat_p, lat_q, hid_p, hid_q,
    s1_send, s1_recv, f_send, f_recv, s2_send, s2_recv,
    g_send, g_recv, y_send, y_recv, c_send, c_recv, l_send, l_recv, h_send, h_recv,
):
    loads = [
        pltpu.make_async_copy(src, dst, in_sem.at[i])
        for i, (src, dst) in enumerate((
            (x_in, x_ref), (w2_in, w2_ref), (w3_in, w3_ref), (w1_in, w1_ref), (gamma_in, gamma_ref),
            (b1_in, b1_ref), (beta_in, beta_ref), (b2_in, b2_ref), (b3_in, b3_ref),
        ))
    ]
    loads[0].start()
    w, n = lax.axis_index("wide"), lax.axis_index("narrow")
    wide = lax.axis_size("wide")
    zh, xx, core = n // 4, n % 4, w % 2
    yy = (w // 2) % 8
    y_up, y_down = w + 2 * ((yy + 1) % 8 - yy), w + 2 * ((yy + 7) % 8 - yy)
    quarter = 2 * core + yy % 2
    has_lo, has_hi = w > 0, w < wide - 1
    lo, hi = jnp.maximum(w - 1, 0), jnp.minimum(w + 1, wide - 1)
    sibling = w + 1 - 2 * core

    def peer(e, d):
        return ((zh + e) % 2) * 4 + (xx + d) % 4

    sent = []

    def send(src, dst, ssem, rsem, device, when=None):
        copy = pltpu.make_async_remote_copy(
            src_ref=src, dst_ref=dst, send_sem=ssem, recv_sem=rsem,
            device_id=device, device_id_type=MESH,
        )
        if when is None:
            copy.start()
        else:
            pl.when(when)(copy.start)
        sent.append((copy, when))

    def arrived(dst, rsem, when=None):
        copy = pltpu.make_async_remote_copy(
            src_ref=dst, dst_ref=dst, send_sem=rsem, recv_sem=rsem,
            device_id=(sibling, n), device_id_type=MESH,
        )
        if when is None:
            copy.wait_recv()
        else:
            pl.when(when)(copy.wait_recv)

    barrier = pltpu.get_barrier_semaphore()
    for e, d in FAR + NEAR:
        pl.semaphore_signal(barrier, inc=1, device_id=(w, peer(e, d)), device_id_type=MESH)

    for y in (y_up, y_down):
        pl.semaphore_signal(barrier, inc=1, device_id=(y, n), device_id_type=MESH)

    @pl.when(has_lo)
    def _():
        pl.semaphore_signal(barrier, inc=1, device_id=(lo, n), device_id_type=MESH)

    @pl.when(has_hi)
    def _():
        pl.semaphore_signal(barrier, inc=1, device_id=(hi, n), device_id_type=MESH)

    i, j = iota((256, 256), 0), iota((256, 256), 1)
    source = ((i >> 4) & 3) * 64 + (i >> 7) * 32 + (i & 15) * 2 + ((i >> 6) & 1)
    perm = jnp.where(j == source, 1.0, 0.0).astype(BF16)
    loads[0].wait()
    for load in loads[1:]:
        load.start()
    cut = [
        jnp.dot(perm, x_ref[256 * z : 256 * z + 256, :], preferred_element_type=F32)
        for z in range(2)
    ]
    parts = [
        jnp.concatenate([cut[z][64 * t : 64 * t + 64] for z in range(2)], axis=0) for t in range(4)
    ]
    blank = jnp.zeros((128, 64), F32)
    turned = [
        pltpu.roll(jnp.concatenate([parts[t], blank], axis=1), 24 * t, 1) if t else
        jnp.concatenate([parts[t], blank], axis=1)
        for t in range(4)
    ]
    lane = iota((128, 256), 1)
    for m in range(8):
        at = (lane - 24 * m) & 255
        block = jnp.where(at < 24, turned[0], jnp.where(at < 48, turned[1], jnp.where(at < 72, turned[2], turned[3])))
        block = pltpu.roll(block, (256 - 24 * m) % 256, 1)[:, :128] if m else block[:, :128]
        block = jnp.where(lane[:, :128] < 96, block, 0.0)
        first, second = block[:64], pltpu.roll(block[64:], 96, 1)
        ln = iota((64, 128), 1)
        rest = jnp.where(ln[:32] < 64, second[:32], pltpu.roll(second[32:], 64, 1))
        send1[m] = jnp.concatenate([jnp.where(ln < 96, first, second), rest], axis=0).astype(BF16)

    pl.semaphore_wait(barrier, 9 + has_lo.astype(jnp.int32) + has_hi.astype(jnp.int32))

    for e, d in FAR + NEAR:
        m = peer(e, d)
        send(send1.at[m], recv1.at[n], s1_send.at[m], s1_recv.at[n], (w, m))
    recv1[n] = send1[n]

    for load in loads[1:]:
        load.wait()

    def stage(layer, ref):

        @pl.loop(0, 11)
        def _(t):
            at = 11 * quarter + t
            tap, kind = 2 * (at // 3), at % 3
            even = ref[jnp.minimum(tap, 26)].astype(F32)
            odd = ref[jnp.minimum(tap + 1, 26)].astype(F32)
            odd = jnp.where(tap + 1 < 27, odd, 0.0)
            both = jnp.concatenate([even[:, 128:], odd[:, 128:]], axis=1)
            value = jnp.where(kind == 0, even[:, :128], jnp.where(kind == 1, odd[:, :128], both))
            wts[layer, at, n] = value.astype(BF16)

    mirror = peer(1, 0)

    def slice_of(layer, m):
        return wts.at[layer, pl.ds(11 * quarter, 11), m]

    def to_peers(layer):
        part = slice_of(layer, n)
        for at, (e, d) in enumerate(((1, 0),) + NEAR):
            send(part, part, g_send.at[layer, at], g_recv.at[layer, n], (w, peer(e, d)))

    def forward(layer):
        part = slice_of(layer, mirror)
        arrived(part, g_recv.at[layer, mirror])
        for at, (e, d) in enumerate(NEAR):
            send(part, part, g_send.at[layer, 4 + at], g_recv.at[layer, mirror], (w, peer(e, d)))

    def y_part(layer, q, up, half):
        return wts.at[layer, pl.ds(11 * q + (0 if up else 6), 6 if up else 5), pl.ds(4 * half, 4)]

    def along_y(layer, turn):
        for e, d in NEAR if turn == 0 else FAR[:3]:
            m = peer(e, d)
            arrived(slice_of(layer, m), g_recv.at[layer, m])
        half = (zh + turn) % 2
        for up, y in ((1, y_up), (0, y_down)):
            part = y_part(layer, quarter, up, half)
            send(part, part, y_send.at[layer, turn, up], y_recv.at[layer, turn, up], (y, n))

    def to_sibling(layer):
        for turn in range(2):
            for up in (1, 0):
                part = y_part(layer, quarter + 1 - 2 * (yy % 2), up, (zh + turn) % 2)
                arrived(part, y_recv.at[layer, turn, up])
        part = wts.at[layer, pl.ds(22 * core, 22)]
        send(part, part, c_send.at[layer], c_recv.at[layer], (sibling, n))

    for layer, ref in ((0, w2_ref), (1, w3_ref)):
        stage(layer, ref)
        to_peers(layer)

    w1k[...] = jnp.zeros_like(w1k)

    def fill(a, odd):
        for b in range(5):
            step, rp = b // 2, b % 2
            at = a * 3 + step
            v = w1_ref[a * 5 + b].astype(F32)
            last = jnp.concatenate([v[96:120], jnp.zeros((8, 192), F32)], axis=0)
            for base, rows in ((0, v[0:48]), (128, v[48:96])):
                rows = rows.astype(BF16)
                if not odd:
                    w1k[at, base + 48 * rp : base + 48 * rp + 48, 0:192] = rows
                elif rp == 0:
                    w1k[at, base + 96 : base + 128, 0:192] = rows[0:32]
                    w1k[at, base : base + 16, 0:192] = rows[32:48]
                else:
                    w1k[at, base + 16 : base + 64, 0:192] = rows
            gap = 128 * rp + (64 if odd else 96)
            w1k[at, gap : gap + 32, 0:192] = last.astype(BF16)

    @pl.loop(0, 3)
    def _(t):
        fill(2 * t, False)

    @pl.loop(0, 2)
    def _(t):
        fill(2 * t + 1, True)

    planes[:, 0:16, :] = jnp.zeros((5, 16, 256), BF16)
    planes[:, 528:544, :] = jnp.zeros((5, 16, 256), BF16)
    acc[0:32, :] = jnp.zeros((32, 256), F32)
    acc[544:576, :] = jnp.zeros((32, 256), F32)

    for turn in range(2):
        for e, d in NEAR if turn == 0 else FAR:
            m = peer(e, d)
            arrived(recv1.at[m], s1_recv.at[m])
        g = (zh + turn) % 2
        four = pl.ds(4 * g, 4)
        send(recv1.at[four], from_lo.at[four], f_send.at[0, turn], f_recv.at[0, g], (hi, n), has_hi)
        send(
            recv1.at[four, 0:64], from_hi.at[four], f_send.at[1, turn], f_recv.at[1, g], (lo, n), has_lo
        )

    def build(a, read, begin=0, count=8):
        @pl.loop(0, count, unroll=count // 2)
        def _(step):
            blk = begin + step
            x = read(blk).astype(F32)
            ln = iota((64, 128), 1)
            kept = ln < 96
            if a % 2:
                rest = jnp.concatenate([x[64:], pltpu.roll(x[64:], 64, 1)], axis=0)
                x = jnp.where(kept, rest, x[:64])
                kept = (ln < 64) | (ln >= 96)
            after = rows_shifted(x, 1)
            before = jnp.where(kept, rows_shifted(x, -1), pltpu.roll(after, 96, 1))
            same = jnp.where(kept, x, pltpu.roll(after, 48, 1))
            at = pl.ds(pl.multiple_of(16 + 64 * blk, 16), 64)
            planes[a, at, 0:128] = before.astype(BF16)
            planes[a, at, 128:256] = same.astype(BF16)

    def product(a, first=0, size=512):
        rows = jnp.concatenate(
            [planes[a, pl.ds(first + 16 * s, size), :] for s in range(3)], axis=1
        )
        return jnp.dot(
            rows, w1k[3 * a : 3 * a + 3].reshape(768, 256), preferred_element_type=F32
        )

    along_y(0, 0)
    build(2, lambda blk: recv1[blk, 0:64])
    build(3, lambda blk: recv1[blk])
    acc[32:544, :] = product(2) + product(3)

    @pl.when(jnp.logical_not(has_lo))
    def _():
        from_lo[...] = jnp.zeros_like(from_lo)

    @pl.when(jnp.logical_not(has_hi))
    def _():
        from_hi[...] = jnp.zeros_like(from_hi)

    for turn in range(2):
        g = (zh + turn) % 2
        four = pl.ds(4 * g, 4)
        if turn == 0:
            forward(0)
        size = (240, 272)[turn]
        first = pl.multiple_of(zh * 272 if turn == 0 else (1 - zh) * 240, 16)
        target = pl.ds(pl.multiple_of(32 + first, 16), size)

        def use_lo(g=g, four=four, first=first, size=size, target=target):
            arrived(from_lo.at[four], f_recv.at[0, g], has_lo)
            build(0, lambda blk: from_lo[blk, 0:64], 4 * g, 4)
            build(1, lambda blk: from_lo[blk], 4 * g, 4)
            acc[target, :] += product(0, first, size) + product(1, first, size)

        def use_hi(g=g, four=four, first=first, size=size, target=target):
            arrived(from_hi.at[four], f_recv.at[1, g], has_hi)
            build(4, lambda blk: from_hi[blk], 4 * g, 4)
            acc[target, :] += product(4, first, size)

        @pl.when(core == 0)
        def _():
            use_hi()
            use_lo()

        @pl.when(core == 1)
        def _():
            use_lo()
            use_hi()

    def packed(at):
        rows = acc[at, :]
        left, right = rows[:, :128], rows[:, 128:]
        ln = iota((64, 128), 1)
        side = jnp.where(ln < 64, right[:64], pltpu.roll(right[64:], 64, 1))
        return jnp.concatenate([left, side], axis=0)

    for e, d in FAR + NEAR:
        m = peer(e, d)
        send2[m] = packed(pl.ds(pl.multiple_of(64 * m, 64), 128)).astype(BF16)
        send(send2.at[m], recv2.at[n], s2_send.at[m], s2_recv.at[n], (w, m))
    forward(1)
    along_y(1, 0)
    along_y(0, 1)
    along_y(1, 1)
    to_sibling(0)

    total = packed(pl.ds(pl.multiple_of(64 * n, 64), 128))
    for e, d in NEAR + FAR:
        m = peer(e, d)
        arrived(recv2.at[m], s2_recv.at[m])
        total = total + recv2[m].astype(F32)
    side = total[128:192]
    side = jnp.concatenate([side, pltpu.roll(side, 64, 1)], axis=0)
    conv = jnp.concatenate([total[:128], side[:, :64]], axis=1) + b1_ref[...]
    denom = beta_ref[...] + jnp.dot(
        conv * conv, gamma_ref[...], precision=lax.Precision.HIGHEST, preferred_element_type=F32
    )
    latent = (conv * lax.rsqrt(denom)).astype(BF16)

    def inside(values, first):
        row = first + (iota(values.shape, 0) >> 4)
        return jnp.where((row >= 0) & (row < 32), values, 0.0).astype(BF16)

    def exchange(buf, ssem, rsem):
        send(buf.at[1], buf.at[0], ssem.at[0], rsem.at[0], (hi, n), has_hi)
        send(buf.at[1], buf.at[2], ssem.at[1], rsem.at[1], (lo, n), has_lo)

    def kernel_of(layer, at):
        return wts[layer, at].reshape(192, 128)

    def layer_of(layer, buf, buf_q, rsem, rows):
        def shifts(z):
            x = buf[z].astype(F32)
            buf_q[z, 0] = rows_shifted(x, -1).astype(BF16)
            buf_q[z, 1] = rows_shifted(x, 1).astype(BF16)

        sums = [jnp.zeros((rows, 256), F32)] * 2

        def taps(z, first):
            for j in range(9):
                b, c = j // 3, j % 3
                at = pl.ds(16 * b, rows)
                left = buf[z, at, :] if c == 1 else buf_q[z, c // 2, at, :]
                if z is one:
                    pair, odd = (9 + j) // 2, (9 + j) % 2
                else:
                    pair, odd = first + j // 2, j % 2
                kern = jnp.concatenate(
                    [kernel_of(layer, 3 * pair + odd), kernel_of(layer, 3 * pair + 2)], axis=1
                )
                sums[odd] += jnp.dot(left, kern, preferred_element_type=F32)

        one = 1
        shifts(one)
        taps(one, None)
        near = 2 * (1 - core)
        far = 2 - near
        has_far = jnp.where(core == 0, has_lo.astype(jnp.int32), has_hi.astype(jnp.int32)) == 1

        @pl.when(jnp.logical_not(has_far))
        def _():
            buf[far] = jnp.zeros((buf.shape[1], 192), BF16)

        arrived(buf.at[near], rsem.at[1 - core])
        shifts(near)
        taps(near, 9 * (1 - core))
        if layer == 0:
            to_sibling(1)
        arrived(buf.at[far], rsem.at[core], has_far)
        shifts(far)
        taps(far, 9 * core)
        even, odd = sums
        side = even[:, 128:] + pltpu.roll(odd[:, 128:], 64, 1)
        return jnp.concatenate([even[:, :128] + odd[:, :128], side[:, :64]], axis=1)

    lat_p[1] = inside(jnp.abs(latent.astype(F32)), 4 * n - 2)
    exchange(lat_p, l_send, l_recv)
    lat_ref[...] = latent[32:96]
    other = pl.ds(22 * (1 - core), 22)
    arrived(wts.at[0, other], c_recv.at[0])
    hidden = jnp.maximum(layer_of(0, lat_p, lat_q, l_recv, 96) + b2_ref[...], 0.0)
    hid_p[1] = inside(hidden, 4 * n - 1)
    exchange(hid_p, h_send, h_recv)
    arrived(wts.at[1, other], c_recv.at[1])
    s = layer_of(1, hid_p, hid_q, h_recv, 64) + b3_ref[...]
    sc_ref[...] = s

    for copy, when in sent:
        if when is None:
            copy.wait_send()
        else:
            pl.when(when)(copy.wait_send)


def finish(lat_in, s_in, lat_ref, sc_ref):
    lat_ref[...] = lat_in[...]
    s = s_in[...]
    sc_ref[...] = 0.11 + (jnp.maximum(s, 0.0) + jnp.log1p(jnp.exp(-jnp.abs(s))))


def on_device(density, w1, b1, beta, gamma, w2, b2, w3, b3):
    vmem = pl.BlockSpec(memory_space=pltpu.VMEM)
    dma = pltpu.SemaphoreType.DMA
    latent, scales = pl.pallas_call(
        kernel,
        out_shape=(
            jax.ShapeDtypeStruct((64, 192), BF16),
            jax.ShapeDtypeStruct((64, 192), F32),
        ),
        in_specs=[pl.BlockSpec(memory_space=pl.ANY)] * 9,
        out_specs=(vmem, vmem),
        scratch_shapes=[
            pltpu.VMEM((512, 192), BF16),
            pltpu.VMEM((25, 120, 192), BF16),
            pltpu.VMEM((1, 192), F32),
            pltpu.VMEM((1, 192), F32),
            pltpu.VMEM((192, 192), F32),
            pltpu.VMEM((27, 24, 192), BF16),
            pltpu.VMEM((1, 192), F32),
            pltpu.VMEM((27, 24, 192), BF16),
            pltpu.VMEM((1, 192), F32),
            dma((9,)),
            pltpu.VMEM((8, 96, 128), BF16),
            pltpu.VMEM((8, 96, 128), BF16),
            pltpu.VMEM((8, 96, 128), BF16),
            pltpu.VMEM((8, 64, 128), BF16),
            pltpu.VMEM((5, 544, 256), BF16),
            pltpu.VMEM((15, 256, 256), BF16),
            pltpu.VMEM((576, 256), F32),
            pltpu.VMEM((8, 192, 128), BF16),
            pltpu.VMEM((8, 192, 128), BF16),
            pltpu.VMEM((2, 44, 8, 24, 128), BF16),
            pltpu.VMEM((3, 128, 192), BF16),
            pltpu.VMEM((3, 2, 128, 192), BF16),
            pltpu.VMEM((3, 96, 192), BF16),
            pltpu.VMEM((3, 2, 96, 192), BF16),
            dma((8,)), dma((8,)),
            dma((2, 2)), dma((2, 2)),
            dma((8,)), dma((8,)),
            dma((2, 7)), dma((2, 8)),
            dma((2, 2, 2)), dma((2, 2, 2)),
            dma((2,)), dma((2,)),
            dma((2,)), dma((2,)),
            dma((2,)), dma((2,)),
        ],
        compiler_params=pltpu.CompilerParams(
            collective_id=0, has_side_effects=True, vmem_limit_bytes=60 * 2**20
        ),
    )(
        density.reshape(512, 192),
        w1.reshape(25, 120, 192),
        b1.reshape(1, 192),
        beta.reshape(1, 192),
        gamma,
        w2.reshape(27, 24, 192),
        b2.reshape(1, 192),
        w3.reshape(27, 24, 192),
        b3.reshape(1, 192),
    )
    latent, scales = pl.pallas_call(
        finish,
        out_shape=(
            jax.ShapeDtypeStruct((64, 192), BF16),
            jax.ShapeDtypeStruct((64, 192), F32),
        ),
        in_specs=[vmem] * 2,
        out_specs=(vmem, vmem),
    )(latent, scales)
    return latent.reshape(1, 4, 16, 192), scales.reshape(1, 4, 16, 192)


def solution(mesh):
    in_specs = (
        P("wide", "narrow", None, None),
        P(None, None, None, "narrow", None),
        P(),
        P(),
        P(),
        P(None, None, None, "narrow", None),
        P(),
        P(None, None, None, "narrow", None),
        P(),
    )
    out_specs = (P("wide", "narrow", None, None), P("wide", "narrow", None, None))
    return jax.shard_map(
        on_device, mesh=mesh, in_specs=in_specs, out_specs=out_specs, check_vma=False
    )
```

```python
import jax
import jax.numpy as jnp
from jax import lax
from jax.experimental import pallas as pl
from jax.experimental.pallas import tpu as pltpu
from jax.sharding import PartitionSpec as P

MESH = pl.DeviceIdType.MESH
F32 = jnp.float32
BF16 = jnp.bfloat16

FAR = ((1, 2), (1, 1), (1, 3), (1, 0))
NEAR = ((0, 2), (0, 1), (0, 3))


def iota(shape, dim):
    return lax.broadcasted_iota(jnp.int32, shape, dim)


def rows_shifted(x, by):
    n = x.shape[0]
    col = iota(x.shape, 0) & 15
    if by == -1:
        return jnp.where(col == 0, 0.0, pltpu.roll(x, 1, 0))
    return jnp.where(col == 15, 0.0, pltpu.roll(x, n - 1, 0))


def kernel(
    x_in, w1_in, b1_in, beta_in, gamma_in, w2_in, b2_in, w3_in, b3_in,
    lat_ref, sc_ref,
    x_ref, w1_ref, b1_ref, beta_ref, gamma_ref, w2_ref, b2_ref, w3_ref, b3_ref, in_sem,
    send1, recv1, from_lo, from_hi, planes, w1k, acc, send2, recv2, wts,
    lat_p, lat_q, hid_p, hid_q,
    s1_send, s1_recv, f_send, f_recv, s2_send, s2_recv,
    g_send, g_recv, y_send, y_recv, c_send, c_recv, l_send, l_recv, h_send, h_recv,
):
    loads = [
        pltpu.make_async_copy(src, dst, in_sem.at[i])
        for i, (src, dst) in enumerate((
            (x_in, x_ref), (w2_in, w2_ref), (w3_in, w3_ref), (w1_in, w1_ref), (gamma_in, gamma_ref),
            (b1_in, b1_ref), (beta_in, beta_ref), (b2_in, b2_ref), (b3_in, b3_ref),
        ))
    ]
    loads[0].start()
    w, n = lax.axis_index("wide"), lax.axis_index("narrow")
    wide = lax.axis_size("wide")
    zh, xx, core = n // 4, n % 4, w % 2
    yy = (w // 2) % 8
    y_up, y_down = w + 2 * ((yy + 1) % 8 - yy), w + 2 * ((yy + 7) % 8 - yy)
    quarter = 2 * core + yy % 2
    has_lo, has_hi = w > 0, w < wide - 1
    lo, hi = jnp.maximum(w - 1, 0), jnp.minimum(w + 1, wide - 1)
    sibling = w + 1 - 2 * core

    def peer(e, d):
        return ((zh + e) % 2) * 4 + (xx + d) % 4

    sent = []

    def send(src, dst, ssem, rsem, device, when=None):
        copy = pltpu.make_async_remote_copy(
            src_ref=src, dst_ref=dst, send_sem=ssem, recv_sem=rsem,
            device_id=device, device_id_type=MESH,
        )
        if when is None:
            copy.start()
        else:
            pl.when(when)(copy.start)
        sent.append((copy, when))

    def arrived(dst, rsem, when=None):
        copy = pltpu.make_async_remote_copy(
            src_ref=dst, dst_ref=dst, send_sem=rsem, recv_sem=rsem,
            device_id=(sibling, n), device_id_type=MESH,
        )
        if when is None:
            copy.wait_recv()
        else:
            pl.when(when)(copy.wait_recv)

    barrier = pltpu.get_barrier_semaphore()
    for e, d in FAR + NEAR:
        pl.semaphore_signal(barrier, inc=1, device_id=(w, peer(e, d)), device_id_type=MESH)

    for y in (y_up, y_down):
        pl.semaphore_signal(barrier, inc=1, device_id=(y, n), device_id_type=MESH)

    @pl.when(has_lo)
    def _():
        pl.semaphore_signal(barrier, inc=1, device_id=(lo, n), device_id_type=MESH)

    @pl.when(has_hi)
    def _():
        pl.semaphore_signal(barrier, inc=1, device_id=(hi, n), device_id_type=MESH)

    i, j = iota((256, 256), 0), iota((256, 256), 1)
    source = ((i >> 4) & 3) * 64 + (i >> 7) * 32 + (i & 15) * 2 + ((i >> 6) & 1)
    perm = jnp.where(j == source, 1.0, 0.0).astype(BF16)
    loads[0].wait()
    for load in loads[1:]:
        load.start()
    cut = [
        jnp.dot(perm, x_ref[256 * z : 256 * z + 256, :], preferred_element_type=F32)
        for z in range(2)
    ]
    parts = [
        jnp.concatenate([cut[z][64 * t : 64 * t + 64] for z in range(2)], axis=0) for t in range(4)
    ]
    blank = jnp.zeros((128, 64), F32)
    turned = [
        pltpu.roll(jnp.concatenate([parts[t], blank], axis=1), 24 * t, 1) if t else
        jnp.concatenate([parts[t], blank], axis=1)
        for t in range(4)
    ]
    lane = iota((128, 256), 1)
    for m in range(8):
        at = (lane - 24 * m) & 255
        block = jnp.where(at < 24, turned[0], jnp.where(at < 48, turned[1], jnp.where(at < 72, turned[2], turned[3])))
        block = pltpu.roll(block, (256 - 24 * m) % 256, 1)[:, :128] if m else block[:, :128]
        block = jnp.where(lane[:, :128] < 96, block, 0.0)
        first, second = block[:64], pltpu.roll(block[64:], 96, 1)
        ln = iota((64, 128), 1)
        rest = jnp.where(ln[:32] < 64, second[:32], pltpu.roll(second[32:], 64, 1))
        send1[m] = jnp.concatenate([jnp.where(ln < 96, first, second), rest], axis=0).astype(BF16)

    pl.semaphore_wait(barrier, 9 + has_lo.astype(jnp.int32) + has_hi.astype(jnp.int32))

    for e, d in FAR + NEAR:
        m = peer(e, d)
        send(send1.at[m], recv1.at[n], s1_send.at[m], s1_recv.at[n], (w, m))
    recv1[n] = send1[n]

    for load in loads[1:]:
        load.wait()

    def stage(layer, ref):

        @pl.loop(0, 11)
        def _(t):
            at = 11 * quarter + t
            tap, kind = 2 * (at // 3), at % 3
            even = ref[jnp.minimum(tap, 26)].astype(F32)
            odd = ref[jnp.minimum(tap + 1, 26)].astype(F32)
            odd = jnp.where(tap + 1 < 27, odd, 0.0)
            both = jnp.concatenate([even[:, 128:], odd[:, 128:]], axis=1)
            value = jnp.where(kind == 0, even[:, :128], jnp.where(kind == 1, odd[:, :128], both))
            wts[layer, at, n] = value.astype(BF16)

    mirror = peer(1, 0)

    def slice_of(layer, m):
        return wts.at[layer, pl.ds(11 * quarter, 11), m]

    def to_peers(layer):
        part = slice_of(layer, n)
        for at, (e, d) in enumerate(((1, 0),) + NEAR):
            send(part, part, g_send.at[layer, at], g_recv.at[layer, n], (w, peer(e, d)))

    def forward(layer):
        part = slice_of(layer, mirror)
        arrived(part, g_recv.at[layer, mirror])
        for at, (e, d) in enumerate(NEAR):
            send(part, part, g_send.at[layer, 4 + at], g_recv.at[layer, mirror], (w, peer(e, d)))

    def y_part(layer, q, up, half):
        return wts.at[layer, pl.ds(11 * q + (0 if up else 6), 6 if up else 5), pl.ds(4 * half, 4)]

    def along_y(layer, turn):
        for e, d in NEAR if turn == 0 else FAR[:3]:
            m = peer(e, d)
            arrived(slice_of(layer, m), g_recv.at[layer, m])
        half = (zh + turn) % 2
        for up, y in ((1, y_up), (0, y_down)):
            part = y_part(layer, quarter, up, half)
            send(part, part, y_send.at[layer, turn, up], y_recv.at[layer, turn, up], (y, n))

    def to_sibling(layer):
        for turn in range(2):
            for up in (1, 0):
                part = y_part(layer, quarter + 1 - 2 * (yy % 2), up, (zh + turn) % 2)
                arrived(part, y_recv.at[layer, turn, up])
        part = wts.at[layer, pl.ds(22 * core, 22)]
        send(part, part, c_send.at[layer], c_recv.at[layer], (sibling, n))

    for layer, ref in ((0, w2_ref), (1, w3_ref)):
        stage(layer, ref)
        to_peers(layer)

    w1k[...] = jnp.zeros_like(w1k)

    def fill(a, odd):
        for b in range(5):
            step, rp = b // 2, b % 2
            at = a * 3 + step
            v = w1_ref[a * 5 + b].astype(F32)
            last = jnp.concatenate([v[96:120], jnp.zeros((8, 192), F32)], axis=0)
            for base, rows in ((0, v[0:48]), (128, v[48:96])):
                rows = rows.astype(BF16)
                if not odd:
                    w1k[at, base + 48 * rp : base + 48 * rp + 48, 0:192] = rows
                elif rp == 0:
                    w1k[at, base + 96 : base + 128, 0:192] = rows[0:32]
                    w1k[at, base : base + 16, 0:192] = rows[32:48]
                else:
                    w1k[at, base + 16 : base + 64, 0:192] = rows
            gap = 128 * rp + (64 if odd else 96)
            w1k[at, gap : gap + 32, 0:192] = last.astype(BF16)

    @pl.loop(0, 3)
    def _(t):
        fill(2 * t, False)

    @pl.loop(0, 2)
    def _(t):
        fill(2 * t + 1, True)

    planes[:, 0:16, :] = jnp.zeros((5, 16, 256), BF16)
    planes[:, 528:544, :] = jnp.zeros((5, 16, 256), BF16)
    acc[0:32, :] = jnp.zeros((32, 256), F32)
    acc[544:576, :] = jnp.zeros((32, 256), F32)

    for turn in range(2):
        for e, d in NEAR if turn == 0 else FAR:
            m = peer(e, d)
            arrived(recv1.at[m], s1_recv.at[m])
        g = (zh + turn) % 2
        four = pl.ds(4 * g, 4)
        send(recv1.at[four], from_lo.at[four], f_send.at[0, turn], f_recv.at[0, g], (hi, n), has_hi)
        send(
            recv1.at[four, 0:64], from_hi.at[four], f_send.at[1, turn], f_recv.at[1, g], (lo, n), has_lo
        )

    def build(a, read, begin=0, count=8):
        @pl.loop(0, count, unroll=count // 2)
        def _(step):
            blk = begin + step
            x = read(blk).astype(F32)
            ln = iota((64, 128), 1)
            kept = ln < 96
            if a % 2:
                rest = jnp.concatenate([x[64:], pltpu.roll(x[64:], 64, 1)], axis=0)
                x = jnp.where(kept, rest, x[:64])
                kept = (ln < 64) | (ln >= 96)
            after = rows_shifted(x, 1)
            before = jnp.where(kept, rows_shifted(x, -1), pltpu.roll(after, 96, 1))
            same = jnp.where(kept, x, pltpu.roll(after, 48, 1))
            at = pl.ds(pl.multiple_of(16 + 64 * blk, 16), 64)
            planes[a, at, 0:128] = before.astype(BF16)
            planes[a, at, 128:256] = same.astype(BF16)

    def product(a, first=0, size=512):
        rows = jnp.concatenate(
            [planes[a, pl.ds(first + 16 * s, size), :] for s in range(3)], axis=1
        )
        return jnp.dot(
            rows, w1k[3 * a : 3 * a + 3].reshape(768, 256), preferred_element_type=F32
        )

    along_y(0, 0)
    build(2, lambda blk: recv1[blk, 0:64])
    build(3, lambda blk: recv1[blk])
    acc[32:544, :] = product(2) + product(3)

    @pl.when(jnp.logical_not(has_lo))
    def _():
        from_lo[...] = jnp.zeros_like(from_lo)

    @pl.when(jnp.logical_not(has_hi))
    def _():
        from_hi[...] = jnp.zeros_like(from_hi)

    for turn in range(2):
        g = (zh + turn) % 2
        four = pl.ds(4 * g, 4)
        arrived(from_lo.at[four], f_recv.at[0, g], has_lo)
        arrived(from_hi.at[four], f_recv.at[1, g], has_hi)
        if turn == 0:
            forward(0)
        build(0, lambda blk: from_lo[blk, 0:64], 4 * g, 4)
        build(1, lambda blk: from_lo[blk], 4 * g, 4)
        build(4, lambda blk: from_hi[blk], 4 * g, 4)
        size = (240, 272)[turn]
        first = pl.multiple_of(zh * 272 if turn == 0 else (1 - zh) * 240, 16)
        add = product(0, first, size) + product(1, first, size) + product(4, first, size)
        acc[pl.ds(pl.multiple_of(32 + first, 16), size), :] += add

    def packed(at):
        rows = acc[at, :]
        left, right = rows[:, :128], rows[:, 128:]
        ln = iota((64, 128), 1)
        side = jnp.where(ln < 64, right[:64], pltpu.roll(right[64:], 64, 1))
        return jnp.concatenate([left, side], axis=0)

    for e, d in FAR + NEAR:
        m = peer(e, d)
        send2[m] = packed(pl.ds(pl.multiple_of(64 * m, 64), 128)).astype(BF16)
        send(send2.at[m], recv2.at[n], s2_send.at[m], s2_recv.at[n], (w, m))
    forward(1)
    along_y(1, 0)
    along_y(0, 1)
    along_y(1, 1)
    to_sibling(0)

    total = packed(pl.ds(pl.multiple_of(64 * n, 64), 128))
    for e, d in NEAR + FAR:
        m = peer(e, d)
        arrived(recv2.at[m], s2_recv.at[m])
        total = total + recv2[m].astype(F32)
    side = total[128:192]
    side = jnp.concatenate([side, pltpu.roll(side, 64, 1)], axis=0)
    conv = jnp.concatenate([total[:128], side[:, :64]], axis=1) + b1_ref[...]
    denom = beta_ref[...] + jnp.dot(
        conv * conv, gamma_ref[...], precision=lax.Precision.HIGHEST, preferred_element_type=F32
    )
    latent = (conv * lax.rsqrt(denom)).astype(BF16)

    def inside(values, first):
        row = first + (iota(values.shape, 0) >> 4)
        return jnp.where((row >= 0) & (row < 32), values, 0.0).astype(BF16)

    def exchange(buf, ssem, rsem):
        send(buf.at[1], buf.at[0], ssem.at[0], rsem.at[0], (hi, n), has_hi)
        send(buf.at[1], buf.at[2], ssem.at[1], rsem.at[1], (lo, n), has_lo)

    def kernel_of(layer, at):
        return wts[layer, at].reshape(192, 128)

    def layer_of(layer, buf, buf_q, rsem, rows):
        def shifts(z):
            x = buf[z].astype(F32)
            buf_q[z, 0] = rows_shifted(x, -1).astype(BF16)
            buf_q[z, 1] = rows_shifted(x, 1).astype(BF16)

        sums = [jnp.zeros((rows, 256), F32)] * 2

        def taps(z, first):
            for j in range(9):
                b, c = j // 3, j % 3
                at = pl.ds(16 * b, rows)
                left = buf[z, at, :] if c == 1 else buf_q[z, c // 2, at, :]
                if z is one:
                    pair, odd = (9 + j) // 2, (9 + j) % 2
                else:
                    pair, odd = first + j // 2, j % 2
                kern = jnp.concatenate(
                    [kernel_of(layer, 3 * pair + odd), kernel_of(layer, 3 * pair + 2)], axis=1
                )
                sums[odd] += jnp.dot(left, kern, preferred_element_type=F32)

        one = 1
        shifts(one)
        taps(one, None)
        near = 2 * (1 - core)
        far = 2 - near
        has_far = jnp.where(core == 0, has_lo.astype(jnp.int32), has_hi.astype(jnp.int32)) == 1

        @pl.when(jnp.logical_not(has_far))
        def _():
            buf[far] = jnp.zeros((buf.shape[1], 192), BF16)

        arrived(buf.at[near], rsem.at[1 - core])
        shifts(near)
        taps(near, 9 * (1 - core))
        if layer == 0:
            to_sibling(1)
        arrived(buf.at[far], rsem.at[core], has_far)
        shifts(far)
        taps(far, 9 * core)
        even, odd = sums
        side = even[:, 128:] + pltpu.roll(odd[:, 128:], 64, 1)
        return jnp.concatenate([even[:, :128] + odd[:, :128], side[:, :64]], axis=1)

    lat_p[1] = inside(jnp.abs(latent.astype(F32)), 4 * n - 2)
    exchange(lat_p, l_send, l_recv)
    lat_ref[...] = latent[32:96]
    other = pl.ds(22 * (1 - core), 22)
    arrived(wts.at[0, other], c_recv.at[0])
    hidden = jnp.maximum(layer_of(0, lat_p, lat_q, l_recv, 96) + b2_ref[...], 0.0)
    hid_p[1] = inside(hidden, 4 * n - 1)
    exchange(hid_p, h_send, h_recv)
    arrived(wts.at[1, other], c_recv.at[1])
    s = layer_of(1, hid_p, hid_q, h_recv, 64) + b3_ref[...]
    sc_ref[...] = s

    for copy, when in sent:
        if when is None:
            copy.wait_send()
        else:
            pl.when(when)(copy.wait_send)


def finish(lat_in, s_in, lat_ref, sc_ref):
    lat_ref[...] = lat_in[...]
    s = s_in[...]
    sc_ref[...] = 0.11 + (jnp.maximum(s, 0.0) + jnp.log1p(jnp.exp(-jnp.abs(s))))


def on_device(density, w1, b1, beta, gamma, w2, b2, w3, b3):
    vmem = pl.BlockSpec(memory_space=pltpu.VMEM)
    dma = pltpu.SemaphoreType.DMA
    latent, scales = pl.pallas_call(
        kernel,
        out_shape=(
            jax.ShapeDtypeStruct((64, 192), BF16),
            jax.ShapeDtypeStruct((64, 192), F32),
        ),
        in_specs=[pl.BlockSpec(memory_space=pl.ANY)] * 9,
        out_specs=(vmem, vmem),
        scratch_shapes=[
            pltpu.VMEM((512, 192), BF16),
            pltpu.VMEM((25, 120, 192), BF16),
            pltpu.VMEM((1, 192), F32),
            pltpu.VMEM((1, 192), F32),
            pltpu.VMEM((192, 192), F32),
            pltpu.VMEM((27, 24, 192), BF16),
            pltpu.VMEM((1, 192), F32),
            pltpu.VMEM((27, 24, 192), BF16),
            pltpu.VMEM((1, 192), F32),
            dma((9,)),
            pltpu.VMEM((8, 96, 128), BF16),
            pltpu.VMEM((8, 96, 128), BF16),
            pltpu.VMEM((8, 96, 128), BF16),
            pltpu.VMEM((8, 64, 128), BF16),
            pltpu.VMEM((5, 544, 256), BF16),
            pltpu.VMEM((15, 256, 256), BF16),
            pltpu.VMEM((576, 256), F32),
            pltpu.VMEM((8, 192, 128), BF16),
            pltpu.VMEM((8, 192, 128), BF16),
            pltpu.VMEM((2, 44, 8, 24, 128), BF16),
            pltpu.VMEM((3, 128, 192), BF16),
            pltpu.VMEM((3, 2, 128, 192), BF16),
            pltpu.VMEM((3, 96, 192), BF16),
            pltpu.VMEM((3, 2, 96, 192), BF16),
            dma((8,)), dma((8,)),
            dma((2, 2)), dma((2, 2)),
            dma((8,)), dma((8,)),
            dma((2, 7)), dma((2, 8)),
            dma((2, 2, 2)), dma((2, 2, 2)),
            dma((2,)), dma((2,)),
            dma((2,)), dma((2,)),
            dma((2,)), dma((2,)),
        ],
        compiler_params=pltpu.CompilerParams(
            collective_id=0, has_side_effects=True, vmem_limit_bytes=60 * 2**20
        ),
    )(
        density.reshape(512, 192),
        w1.reshape(25, 120, 192),
        b1.reshape(1, 192),
        beta.reshape(1, 192),
        gamma,
        w2.reshape(27, 24, 192),
        b2.reshape(1, 192),
        w3.reshape(27, 24, 192),
        b3.reshape(1, 192),
    )
    latent, scales = pl.pallas_call(
        finish,
        out_shape=(
            jax.ShapeDtypeStruct((64, 192), BF16),
            jax.ShapeDtypeStruct((64, 192), F32),
        ),
        in_specs=[vmem] * 2,
        out_specs=(vmem, vmem),
    )(latent, scales)
    return latent.reshape(1, 4, 16, 192), scales.reshape(1, 4, 16, 192)


def solution(mesh):
    in_specs = (
        P("wide", "narrow", None, None),
        P(None, None, None, "narrow", None),
        P(),
        P(),
        P(),
        P(None, None, None, "narrow", None),
        P(),
        P(None, None, None, "narrow", None),
        P(),
    )
    out_specs = (P("wide", "narrow", None, None), P("wide", "narrow", None, None))
    return jax.shard_map(
        on_device, mesh=mesh, in_specs=in_specs, out_specs=out_specs, check_vma=False
    )
```
